128 devices in a mesh: gx: 8 (over x, core), gy: 4 (over y), gz: 4 (over z).
Axes of the slice: x: 4, y: 4, z: 4, core: 2. Of those that a mesh axis runs over, the one named last changes fastest.
Arguments:
- field: bfloat16 [64, 32, 32, 512], P(None, 'gx', 'gy', 'gz'), may hold values from -6 to 6
- cotangent: bfloat16 [64, 32, 32, 512], P(None, 'gx', 'gy', 'gz'), may hold values from -6 to 6
- w_fine: bfloat16 [3, 3, 3, 64, 64], replicated, may hold values from -0.15625 to 0.15625
- w_down: bfloat16 [2, 2, 2, 64, 64], replicated, may hold values from -0.25 to 0.25
- w_coarse: bfloat16 [3, 3, 3, 64, 64], replicated, may hold values from -0.15625 to 0.15625
- w_up: bfloat16 [2, 2, 2, 64, 64], replicated, may hold values from -0.75 to 0.75
Outputs:
- grad_field: bfloat16 [64, 32, 32, 512], P(None, 'gx', 'gy', 'gz')
- grad_fine: float32 [3, 3, 3, 64, 64], replicated
- grad_down: float32 [2, 2, 2, 64, 64], replicated
- grad_coarse: float32 [3, 3, 3, 64, 64], replicated
- grad_up: float32 [2, 2, 2, 64, 64], replicated
The draws below stay inside these ranges and needn't reach their ends.
All inputs are finite; a program needn't handle non-finite values.
Results may differ from the reference program's by a relative error of at most 0.008.
Values may be sent and summed in bfloat16 or wider, within the bound.
A program may use at most 64 MiB of HBM per device.

```python
import jax
import jax.numpy as jnp

C = 64
NX = 32
NY = 32
NZ = 512


def steps_of(own_key, dims, pieces, smallest, largest):
    gain = 1.0
    for axis_at, shards_of in pieces:
        steps = jax.random.uniform(jax.random.fold_in(jax.random.fold_in(own_key, 6), axis_at), (shards_of,), jnp.float32, smallest / len(pieces), largest / len(pieces))
        gain = gain * jnp.repeat(jnp.exp(steps), dims[axis_at] // shards_of).reshape((-1,) + (1,) * (len(dims) - 1 - axis_at))
    return gain


def gaussian(key, extent, scale, most, cuts=(), kind=jnp.bfloat16):
    drawn = jax.random.normal(key, extent, jnp.float32) * scale
    if len(cuts) > 0:
        drawn = steps_of(key, extent, cuts, -0.22, 0.18) * drawn
    return jnp.clip(drawn, min=-most, max=most).astype(kind)


def setup_inputs(seed: int = 0) -> dict:
    key_list = jax.random.split(jax.random.key(seed), 7)
    field = gaussian(key_list[0], (C, NX, NY, NZ), 1.0, 6.0, ((1, 8), (2, 4), (3, 4)))
    cotangent = gaussian(key_list[1], (C, NX, NY, NZ), 1.0, 6.0, ((1, 8), (2, 4), (3, 4)))
    w_fine = gaussian(key_list[2], (3, 3, 3, C, C), (27 * C) ** -0.5, 0.15625)
    w_down = gaussian(key_list[3], (2, 2, 2, C, C), (8 * C) ** -0.5, 0.25)
    w_coarse = gaussian(key_list[4], (3, 3, 3, C, C), (27 * C) ** -0.5, 0.15625)
    w_up = gaussian(key_list[5], (2, 2, 2, C, C), C ** -0.5, 0.75)
    return {"field": field, "cotangent": cotangent, "w_fine": w_fine, "w_down": w_down, "w_coarse": w_coarse, "w_up": w_up}


NEG = 0.2

def act(z):
    return NEG * z + (1.0 - NEG) * jax.nn.softplus(z)

def slope(z):
    return NEG + (1.0 - NEG) * jax.nn.sigmoid(z)

def wrapped(v):
    return jnp.pad(v, ((0, 0), (1, 1), (1, 1), (1, 1)), mode='wrap')

def conv_padded(padded, weight):
    size_x, size_y, size_z = (padded.shape[1] - 2, padded.shape[2] - 2, padded.shape[3] - 2)
    total = jnp.zeros((weight.shape[3], size_x, size_y, size_z), jnp.float32)
    for a in range(3):
        for b in range(3):
            for c in range(3):
                piece = padded[:, a:a + size_x, b:b + size_y, c:c + size_z].astype(jnp.float32)
                total = total + jnp.einsum('oi,ixyz->oxyz', weight[a, b, c].astype(jnp.float32), piece)
    return total

def conv_back(padded, weight):
    size_x, size_y, size_z = (padded.shape[1] - 2, padded.shape[2] - 2, padded.shape[3] - 2)
    total = jnp.zeros((weight.shape[4], size_x, size_y, size_z), jnp.float32)
    for a in range(3):
        for b in range(3):
            for c in range(3):
                piece = padded[:, 2 - a:2 - a + size_x, 2 - b:2 - b + size_y, 2 - c:2 - c + size_z].astype(jnp.float32)
                total = total + jnp.einsum('oi,oxyz->ixyz', weight[a, b, c].astype(jnp.float32), piece)
    return total

def filter_terms(grad, padded):
    size_x, size_y, size_z = (grad.shape[1], grad.shape[2], grad.shape[3])
    grad32 = grad.astype(jnp.float32)
    rows = []
    for a in range(3):
        for b in range(3):
            for c in range(3):
                piece = padded[:, a:a + size_x, b:b + size_y, c:c + size_z].astype(jnp.float32)
                rows.append(jnp.einsum('oxyz,ixyz->oi', grad32, piece))
    return jnp.stack(rows).reshape(3, 3, 3, grad.shape[0], padded.shape[0])

def split(v):
    return v.reshape(v.shape[0], v.shape[1] // 2, 2, v.shape[2] // 2, 2, v.shape[3] // 2, 2)

def merge(v):
    return v.reshape(v.shape[0], v.shape[1] * 2, v.shape[3] * 2, v.shape[5] * 2)

def reference(field, cotangent, w_fine, w_down, w_coarse, w_up):
    f32 = jnp.float32
    padded_field = wrapped(field)
    z_fine = conv_padded(padded_field, w_fine)
    h_fine = act(z_fine).astype(jnp.bfloat16)
    z_down = jnp.einsum('abcoi,ixaybzc->oxyz', w_down.astype(f32), split(h_fine).astype(f32))
    d_coarse = act(z_down).astype(jnp.bfloat16)
    padded_coarse = wrapped(d_coarse)
    z_coarse = conv_padded(padded_coarse, w_coarse)
    h_coarse = act(z_coarse).astype(jnp.bfloat16)
    cot_split = split(cotangent).astype(f32)
    g_up = jnp.einsum('abcoi,oxaybzc->ixyz', w_up.astype(f32), cot_split)
    up_sum = jnp.einsum('oxaybzc,ixyz->abcoi', cot_split, h_coarse.astype(f32))
    g_zc = (g_up * slope(z_coarse)).astype(jnp.bfloat16)
    coarse_sum = filter_terms(g_zc, padded_coarse)
    g_d = conv_back(wrapped(g_zc), w_coarse)
    g_zd = (g_d * slope(z_down)).astype(jnp.bfloat16)
    down_sum = jnp.einsum('oxyz,ixaybzc->abcoi', g_zd.astype(f32), split(h_fine).astype(f32))
    g_h = cotangent.astype(f32) + merge(jnp.einsum('abcoi,oxyz->ixaybzc', w_down.astype(f32), g_zd.astype(f32)))
    g_zf = (g_h * slope(z_fine)).astype(jnp.bfloat16)
    fine_sum = filter_terms(g_zf, padded_field)
    grad_field = conv_back(wrapped(g_zf), w_fine).astype(jnp.bfloat16)
    scale = 1.0 / jnp.sqrt(jnp.float32(NX * NY * NZ))
    return (grad_field, fine_sum * scale, down_sum * scale, coarse_sum * scale, up_sum * scale)
```

```python
import functools

import jax
import jax.numpy as jnp
from jax import lax
from jax.experimental import pallas as pl
from jax.experimental.pallas import tpu as pltpu
from jax.sharding import PartitionSpec as P

MESH = pl.DeviceIdType.MESH
F32 = jnp.float32
BF16 = jnp.bfloat16
C = 64
Z = 128
NEG = 0.2

NEAR = [
    (dx, dy, dz)
    for dz in (0, 1, -1)
    for dy in (0, 1, -1)
    for dx in (0, 1, -1)
    if (dx, dy, dz) != (0, 0, 0)
]


def act_slope(z):
    e = jnp.exp(-jnp.abs(z))
    q = 1.0 / (1.0 + e)
    sig = jnp.where(z >= 0.0, q, e * q)
    soft = jnp.maximum(z, 0.0) + jnp.log(1.0 + e)
    return NEG * z + (1.0 - NEG) * soft, NEG + (1.0 - NEG) * sig


def dot(a, b):
    return lax.dot_general(a, b, (((1,), (0,)), ((), ())), preferred_element_type=F32)


def dot_nt(a, b):
    return lax.dot_general(a, b, (((1,), (1,)), ((), ())), preferred_element_type=F32)


def roll(v, shift):
    shift = shift % Z
    return v if shift == 0 else pltpu.roll(v, shift, 1)


def lanes(rows):
    return lax.broadcasted_iota(jnp.int32, (rows, Z), 1)


class Level:
    def __init__(self, nx, ny, step):
        self.nx, self.ny, self.step = nx, ny, step
        self.wide = nx + 2

    def at(self, y, x):
        return self.wide * y + x


def put_own(level, v_ref, y, x, pencil):
    v_ref[y + 1, x, C : 2 * C, :] = pencil
    if x + 1 < level.nx:
        v_ref[y + 1, x + 1, 0:C, :] = pencil
    if x >= 1:
        v_ref[y + 1, x - 1, 2 * C : 3 * C, :] = pencil


def spread_y_halo(level, v_ref):
    for y in (0, level.ny + 1):
        for x in range(level.nx):
            if x + 1 < level.nx:
                v_ref[y, x + 1, 0:C, :] = v_ref[y, x, C : 2 * C, :]
            if x >= 1:
                v_ref[y, x - 1, 2 * C : 3 * C, :] = v_ref[y, x, C : 2 * C, :]


def add_face(level, face, y, x, pencil):
    spot = level.at(y + 1, x + 1)
    return jnp.where(lanes(C) // 2 == spot, roll(pencil, 2 * spot + 1), face)


def pack_face(face, z_send):
    odd = lanes(C // 2) % 2 == 1
    top, bottom = face[: C // 2], face[C // 2 :]
    z_send[0] = jnp.where(odd, top, roll(bottom, -1)).astype(BF16)
    z_send[1] = jnp.where(odd, roll(bottom, 1), top).astype(BF16)


def planes(level, z_recv):
    lane = lanes(C // 2)
    spot = lane // 2
    at_y, at_x = spot // level.wide, spot % level.wide

    def side(value, size, d):
        if d == 1:
            return value == 0
        if d == -1:
            return value == size + 1
        return (value >= 1) & (value <= size)

    packed = []
    for which in range(2):
        total = jnp.zeros((C // 2, Z), F32)
        for n, (dx, dy) in enumerate([(i, j) for j in (0, 1, -1) for i in (0, 1, -1)]):
            shift = -(level.nx * dx) - level.wide * level.ny * dy
            piece = roll(z_recv[which, n].astype(F32), 2 * shift)
            total = jnp.where(side(at_y, level.ny, dy) & side(at_x, level.nx, dx), piece, total)
        packed.append(total)
    low, high = packed
    odd = lane % 2 == 1
    top = jnp.where(odd, roll(low, 1), roll(high, -1))
    bottom = jnp.where(odd, low, high)
    return jnp.concatenate([top, bottom], axis=0)


def halo_columns(level, plane):
    return jnp.concatenate(
        [roll(plane, -2 * (a + level.wide * b)).astype(BF16) for b in range(3) for a in range(3)],
        axis=0,
    )


def stacked(level, v_ref, y):
    return jnp.concatenate(
        [
            jnp.concatenate([v_ref[y + b, x] for x in range(level.nx)], axis=1)
            for b in range(3)
        ],
        axis=0,
    )


def correction(weight, columns):
    p = dot(weight, columns)
    return jnp.where(lanes(C) % 2 == 1, p[:C], p[2 * C :])


def conv_row(level, weight, v_ref, fix, y):
    p = dot(weight, stacked(level, v_ref, y))
    lane = lanes(C)
    row = []
    for x in range(level.nx):
        part = p[:, x * Z : (x + 1) * Z]
        spot = level.at(y, x)
        low = roll(fix, -(2 * spot + 1))
        high = low if level.step == 1 else roll(fix, 126 - 2 * spot)
        left = jnp.where(lane < level.step, low, roll(part[:C], level.step))
        right = jnp.where(lane >= Z - level.step, high, roll(part[2 * C :], -level.step))
        row.append(part[C : 2 * C] + left + right)
    return row


def taps_along_z(level, grad):
    lane = lanes(C)
    first = jnp.where(lane < Z - level.step, roll(grad, -level.step), 0.0)
    last = jnp.where(lane >= level.step, roll(grad, level.step), 0.0)
    return jnp.concatenate([first, grad, last], axis=0).astype(BF16)


def filter_sum(level, g_ref, face, v_ref, columns, total_ref):
    lane = lanes(C)
    own = roll(face, -2 * (level.wide + 1))
    none = jnp.zeros((C, Z), F32)
    edge = jnp.concatenate(
        [jnp.where(lane % 2 == 1, own, 0.0), none, jnp.where(lane % 2 == 0, own, 0.0)], axis=0
    ).astype(BF16)
    total_ref[...] = dot_nt(edge, columns)
    for y in range(level.ny):
        rows = jnp.concatenate([g_ref[y, x] for x in range(level.nx)], axis=1)
        total_ref[...] += dot_nt(rows, stacked(level, v_ref, y))


def kernel(
    sizes,
    field_ref, cot_ref, wf_ref, wd_ref, wc_ref, wu_ref,
    out_ref, of_ref, od_ref, oc_ref, ou_ref,
    w_ff, w_fb, w_cf, w_cb, w_d, w_dt, w_u,
    v_f, v_c, g_c, g_f,
    zs, zr,
    turn, cot, hid, up_grad, slope_f, slope_d, shifted_f, shifted_c, h_two, g_two,
    sum_f, sum_c,
    s_a, s_b, ra_a, ra_b, rb_a, rb_b, rc_a, rc_b,
    near_send, near_recv, sum_send, sum_recv,
):
    cx, cy, cz = sizes
    me = (lax.axis_index("gx"), lax.axis_index("gy"), lax.axis_index("gz"))
    fine, coarse = Level(4, 8, 1), Level(2, 4, 2)

    def device(d):
        return tuple(lax.rem(m + (o % n), n) for m, o, n in zip(me, d, sizes))

    in_plane = [(0, j, k) for j in range(cy) for k in range(cz) if (j, k) != (0, 0)]
    in_line = [(i, 0, 0) for i in range(1, cx)]

    partners = set()
    for d in NEAR + in_plane + in_line:
        partners.add(tuple(o % n for o, n in zip(d, sizes)))
    partners = sorted(partners)
    barrier = pltpu.get_barrier_semaphore()
    for d in partners:
        pl.semaphore_signal(barrier, inc=1, device_id=device(d), device_id_type=MESH)

    started = []

    def exchange(level, which, v_ref):
        copies = []
        for n, (dx, dy, dz) in enumerate(NEAR):
            if dz == 0:
                ny, nx = level.ny, level.nx
                ys = {0: pl.ds(1, ny), 1: pl.ds(ny, 1), -1: pl.ds(1, 1)}[dy]
                yd = {0: pl.ds(1, ny), 1: pl.ds(0, 1), -1: pl.ds(ny + 1, 1)}[dy]
                xs = {0: pl.ds(0, nx), 1: pl.ds(nx - 1, 1), -1: pl.ds(0, 1)}[dx]
                xd = {0: pl.ds(0, nx), 1: pl.ds(0, 1), -1: pl.ds(nx - 1, 1)}[dx]
                rows = pl.ds({0: C, 1: 0, -1: 2 * C}[dx], C)
                src = v_ref.at[ys, xs, pl.ds(C, C), :]
                dst = v_ref.at[yd, xd, rows, :]
            else:
                side = 1 if dz == 1 else 0
                src = zs.at[which, side]
                dst = zr.at[which, 1 - side, (n + 1) % 9]
            copy = pltpu.make_async_remote_copy(
                src_ref=src,
                dst_ref=dst,
                send_sem=near_send.at[which, n],
                recv_sem=near_recv.at[which, n],
                device_id=device((dx, dy, dz)),
                device_id_type=MESH,
            )
            copy.start()
            copies.append(copy)
        started.extend(copies)
        return copies

    def arrive(copies):
        for copy in copies:
            copy.wait_recv()

    face = jnp.zeros((C, Z), F32)
    for x in range(4):
        turn[x] = field_ref[:, x].astype(F32).reshape(C * 8, Z)
        for y in range(8):
            pencil = turn[x, pl.ds(y, C, stride=8), :]
            put_own(fine, v_f, y, x, pencil.astype(BF16))
            face = add_face(fine, face, y, x, pencil)
    pack_face(face, zs.at[0])

    pl.semaphore_wait(barrier, len(partners))
    copies = exchange(fine, 0, v_f)

    eye = (
        lax.broadcasted_iota(jnp.int32, (C, C), 0) == lax.broadcasted_iota(jnp.int32, (C, C), 1)
    ).astype(BF16)

    def flipped(w):
        return dot_nt(eye, w).astype(BF16)

    for w_ref, forward, backward in ((wf_ref, w_ff, w_fb), (wc_ref, w_cf, w_cb)):
        for a in range(3):
            for b in range(3):
                for c in range(3):
                    w = w_ref[a, b, c]
                    m = b * 3 + a
                    forward[c * C : (c + 1) * C, m * C : (m + 1) * C] = w
                    m, k = 8 - m, 2 - c
                    backward[k * C : (k + 1) * C, m * C : (m + 1) * C] = flipped(w)
    for a in range(2):
        for b in range(2):
            for c in range(2):
                m = b * 2 + a
                w = wd_ref[a, b, c]
                w_d[c * C : (c + 1) * C, m * C : (m + 1) * C] = w
                w_dt[m * C : (m + 1) * C, c * C : (c + 1) * C] = flipped(w)
                w_u[c * C : (c + 1) * C, m * C : (m + 1) * C] = flipped(wu_ref[a, b, c])

    for x in range(4):
        turn[x] = cot_ref[:, x].astype(F32).reshape(C * 8, Z)
        for y in range(8):
            m = (y % 2) * 2 + x % 2
            pencil = turn[x, pl.ds(y, C, stride=8), :]
            cot[y // 2, x // 2, m * C : (m + 1) * C, :] = pencil.astype(BF16)

    def pair(ref, y):
        return jnp.concatenate([ref[y, 0], ref[y, 1]], axis=1)

    for y in range(4):
        p = dot(w_u[...], pair(cot, y))
        for x in range(2):
            part = p[:, x * Z : (x + 1) * Z]
            up_grad[y, x] = part[:C] + roll(part[C:], -1)

    arrive(copies)
    spread_y_halo(fine, v_f)
    columns_f = halo_columns(fine, planes(fine, zr.at[0]))
    fix = correction(w_ff[...], columns_f)
    for y in range(8):
        for x, z in enumerate(conv_row(fine, w_ff[...], v_f, fix, y)):
            h, s = act_slope(z)
            m = (y % 2) * 2 + x % 2
            hid[y // 2, x // 2, m * C : (m + 1) * C, :] = h.astype(BF16)
            slope_f[y, x] = s

    even = lanes(C) % 2 == 0
    face = jnp.zeros((C, Z), F32)
    for y in range(4):
        p = dot(w_d[...], pair(hid, y))
        for x in range(2):
            part = p[:, x * Z : (x + 1) * Z]
            d, s = act_slope(part[:C] + roll(part[C:], -1))
            put_own(coarse, v_c, y, x, d.astype(BF16))
            slope_d[y, x] = s
            face = add_face(coarse, face, y, x, jnp.where(even, d, roll(d, 1)))
    pack_face(face, zs.at[1])
    copies = exchange(coarse, 1, v_c)
    arrive(copies)
    spread_y_halo(coarse, v_c)
    columns_c = halo_columns(coarse, planes(coarse, zr.at[1]))
    fix = correction(w_cf[...], columns_c)
    face = jnp.zeros((C, Z), F32)
    for y in range(4):
        for x, z in enumerate(conv_row(coarse, w_cf[...], v_c, fix, y)):
            h, s = act_slope(z)
            h = jnp.where(even, h, 0.0)
            h_two[y, x] = jnp.concatenate([h, roll(h, 1)], axis=0).astype(BF16)
            g = jnp.where(even, up_grad[y, x] * s, 0.0).astype(BF16).astype(F32)
            put_own(coarse, g_c, y, x, g.astype(BF16))
            shifted_c[y, x] = taps_along_z(coarse, g)
            face = add_face(coarse, face, y, x, jnp.where(even, g, roll(g, 1)))
    pack_face(face, zs.at[2])
    copies = exchange(coarse, 2, g_c)

    def long(ref):
        return jnp.concatenate([ref[y, x] for y in range(4) for x in range(2)], axis=1)

    def pack_sums(total_ref, store):
        for c in range(3):
            for q in range(4):
                store(c * 4 + q, total_ref[c * C : (c + 1) * C, q * Z : (q + 1) * Z])
        tail = [total_ref[c * C : (c + 1) * C, 8 * C : 9 * C] for c in range(3)]
        store(12, jnp.concatenate(tail[:2], axis=1))
        store(13, jnp.concatenate([tail[2], jnp.zeros((C, C), F32)], axis=1))

    def place(ref, row):
        chunk = ref.shape[1]
        return row // chunk, pl.ds(row % chunk, 32), slice(None)

    def store(ref, block, value):
        for half in (0, 32):
            ref[place(ref, block * C + half)] = value[half : half + 32].astype(BF16)

    def load(ref, block):
        return jnp.concatenate(
            [ref[place(ref, block * C + half)] for half in (0, 32)], axis=0
        ).astype(F32)

    store_a, store_b = functools.partial(store, s_a), functools.partial(store, s_b)

    filter_sum(coarse, shifted_c, face, v_c, columns_c, sum_c)
    pack_sums(sum_c, store_a)
    p = dot_nt(long(cot), long(h_two))
    for m in range(4):
        store_a(14 + m, p[m * C : (m + 1) * C])

    arrive(copies)
    spread_y_halo(coarse, g_c)
    fix = correction(w_cb[...], halo_columns(coarse, planes(coarse, zr.at[2])))
    for y in range(4):
        for x, g in enumerate(conv_row(coarse, w_cb[...], g_c, fix, y)):
            g = jnp.where(even, g * slope_d[y, x], 0.0)
            g_two[y, x] = jnp.concatenate([g, roll(g, 1)], axis=0).astype(BF16)

    face = jnp.zeros((C, Z), F32)
    for half in range(4):
        p = dot(w_dt[...], pair(g_two, half))
        for b in range(2):
            y = half * 2 + b
            for x in range(4):
                m = b * 2 + x % 2
                wide = p[m * C : (m + 1) * C, (x // 2) * Z : (x // 2 + 1) * Z]
                c = cot[half, x // 2, m * C : (m + 1) * C, :].astype(F32)
                g = ((c + wide) * slope_f[y, x]).astype(BF16).astype(F32)
                put_own(fine, g_f, y, x, g.astype(BF16))
                shifted_f[y, x] = taps_along_z(fine, g)
                face = add_face(fine, face, y, x, g)
    pack_face(face, zs.at[3])
    copies = exchange(fine, 3, g_f)

    p = dot_nt(long(g_two), long(hid))
    for c in range(2):
        for b in range(2):
            store_a(18 + c * 2 + b, p[c * C : (c + 1) * C, b * Z : (b + 1) * Z])
    for block in (22, 23):
        store_a(block, jnp.zeros((C, Z), F32))
    filter_sum(fine, shifted_f, face, v_f, columns_f, sum_f)
    pack_sums(sum_f, store_b)
    for block in (14, 15):
        store_b(block, jnp.zeros((C, Z), F32))

    plane_at = me[1] * cz + me[2]
    voxels = 4 * 8 * Z * cx * cy * cz
    scale = 1.0 / (voxels**0.5)

    def send(src, dst, stage, which, n, d):
        copy = pltpu.make_async_remote_copy(
            src_ref=src,
            dst_ref=dst,
            send_sem=sum_send.at[stage, which, n],
            recv_sem=sum_recv.at[stage, which, n],
            device_id=device(d),
            device_id_type=MESH,
        )
        copy.start()
        started.append(copy)
        return copy

    def scatter(which, s, ra):
        out = []
        for n, d in enumerate(in_plane):
            there = device(d)
            out.append(send(s.at[there[1] * cz + there[2]], ra.at[n], 0, which, n, d))
        return out

    def along(which, s, ra, rb, waits):
        arrive(waits)
        total = s[plane_at].astype(F32)
        for n in range(len(in_plane)):
            total = total + ra[n].astype(F32)
        rb[me[0]] = total.astype(BF16)
        return [send(rb.at[me[0]], rb.at[me[0]], 1, which, n, d) for n, d in enumerate(in_line)]

    def gather(which, rb, rc, waits):
        arrive(waits)
        total = rb[0].astype(F32)
        for n in range(1, cx):
            total = total + rb[n].astype(F32)
        rc[plane_at] = (total * scale).astype(BF16)
        return [send(rc.at[plane_at], rc.at[plane_at], 2, which, n, d) for n, d in enumerate(in_plane)]

    waits_a = scatter(0, s_a, ra_a)
    waits_b = scatter(1, s_b, ra_b)

    arrive(copies)
    spread_y_halo(fine, g_f)
    fix = correction(w_fb[...], halo_columns(fine, planes(fine, zr.at[3])))
    for y in range(8):
        for x, g in enumerate(conv_row(fine, w_fb[...], g_f, fix, y)):
            turn[x, pl.ds(y, C, stride=8), :] = g
    for x in range(4):
        out_ref[:, x] = turn[x].reshape(C, 8, Z).astype(BF16)

    waits_a = along(0, s_a, ra_a, rb_a, waits_a)
    waits_b = along(1, s_b, ra_b, rb_b, waits_b)
    waits_a = gather(0, rb_a, rc_a, waits_a)
    waits_b = gather(1, rb_b, rc_b, waits_b)
    arrive(waits_a)
    arrive(waits_b)

    load_a, load_b = functools.partial(load, rc_a), functools.partial(load, rc_b)

    def unpack_sums(load, o_ref):
        for block in range(14):
            value = load(block)
            for half in range(2):
                if block < 12:
                    c, m = block // 4, (block % 4) * 2 + half
                else:
                    c, m = (block - 12) * 2 + half, 8
                if c < 3:
                    o_ref[m % 3, m // 3, c] = value[:, half * C : (half + 1) * C]

    unpack_sums(load_b, of_ref)
    unpack_sums(load_a, oc_ref)
    for m in range(4):
        value = load_a(14 + m)
        for c in range(2):
            ou_ref[m % 2, m // 2, c] = value[:, c * C : (c + 1) * C]
    for c in range(2):
        for b in range(2):
            value = load_a(18 + c * 2 + b)
            for a in range(2):
                od_ref[a, b, c] = value[:, a * C : (a + 1) * C]

    for copy in started:
        copy.wait_send()


def solution(mesh):
    sizes = (mesh.shape["gx"], mesh.shape["gy"], mesh.shape["gz"])
    cx, cy, cz = sizes
    plane = cy * cz

    def step(field, cotangent, w_fine, w_down, w_coarse, w_up):
        vmem = pl.BlockSpec(memory_space=pltpu.VMEM)
        sums = [
            jax.ShapeDtypeStruct((3, 3, 3, C, C), F32),
            jax.ShapeDtypeStruct((2, 2, 2, C, C), F32),
        ]
        return pl.pallas_call(
            functools.partial(kernel, sizes),
            out_shape=[jax.ShapeDtypeStruct((C, 4, 8, Z), BF16), *sums, *sums],
            in_specs=[vmem] * 6,
            out_specs=[vmem] * 5,
            scratch_shapes=[
                pltpu.VMEM((3 * C, 9 * C), BF16),
                pltpu.VMEM((3 * C, 9 * C), BF16),
                pltpu.VMEM((3 * C, 9 * C), BF16),
                pltpu.VMEM((3 * C, 9 * C), BF16),
                pltpu.VMEM((2 * C, 4 * C), BF16),
                pltpu.VMEM((4 * C, 2 * C), BF16),
                pltpu.VMEM((2 * C, 4 * C), BF16),
                pltpu.VMEM((10, 4, 3 * C, Z), BF16),
                pltpu.VMEM((6, 2, 3 * C, Z), BF16),
                pltpu.VMEM((6, 2, 3 * C, Z), BF16),
                pltpu.VMEM((10, 4, 3 * C, Z), BF16),
                pltpu.VMEM((4, 2, C // 2, Z), BF16),
                pltpu.VMEM((4, 2, 9, C // 2, Z), BF16),
                pltpu.VMEM((4, 8 * C, Z), F32),
                pltpu.VMEM((4, 2, 4 * C, Z), BF16),
                pltpu.VMEM((4, 2, 4 * C, Z), BF16),
                pltpu.VMEM((4, 2, C, Z), F32),
                pltpu.VMEM((8, 4, C, Z), F32),
                pltpu.VMEM((4, 2, C, Z), F32),
                pltpu.VMEM((8, 4, 3 * C, Z), BF16),
                pltpu.VMEM((4, 2, 3 * C, Z), BF16),
                pltpu.VMEM((4, 2, 2 * C, Z), BF16),
                pltpu.VMEM((4, 2, 2 * C, Z), BF16),
                pltpu.VMEM((3 * C, 9 * C), F32),
                pltpu.VMEM((3 * C, 9 * C), F32),
                pltpu.VMEM((plane, 1536 // plane, Z), BF16),
                pltpu.VMEM((plane, 1024 // plane, Z), BF16),
                pltpu.VMEM((plane - 1, 1536 // plane, Z), BF16),
                pltpu.VMEM((plane - 1, 1024 // plane, Z), BF16),
                pltpu.VMEM((cx, 1536 // plane, Z), BF16),
                pltpu.VMEM((cx, 1024 // plane, Z), BF16),
                pltpu.VMEM((plane, 1536 // plane, Z), BF16),
                pltpu.VMEM((plane, 1024 // plane, Z), BF16),
                pltpu.SemaphoreType.DMA((4, 26)),
                pltpu.SemaphoreType.DMA((4, 26)),
                pltpu.SemaphoreType.DMA((3, 2, 15)),
                pltpu.SemaphoreType.DMA((3, 2, 15)),
            ],
            compiler_params=pltpu.CompilerParams(
                collective_id=0, has_side_effects=True, vmem_limit_bytes=48 * 1024 * 1024
            ),
        )(field, cotangent, w_fine, w_down, w_coarse, w_up)

    return jax.shard_map(
        step,
        mesh=mesh,
        in_specs=(P(None, "gx", "gy", "gz"), P(None, "gx", "gy", "gz"), P(), P(), P(), P()),
        out_specs=(P(None, "gx", "gy", "gz"), P(), P(), P(), P()),
        check_vma=False,
    )
```

```python
import functools

import jax
import jax.numpy as jnp
from jax import lax
from jax.experimental import pallas as pl
from jax.experimental.pallas import tpu as pltpu
from jax.sharding import PartitionSpec as P

MESH = pl.DeviceIdType.MESH
F32 = jnp.float32
BF16 = jnp.bfloat16
C = 64
Z = 128
NEG = 0.2

FLAT = [(dx, dy) for dx in (0, 1, -1) for dy in (0, 1, -1)]

SIDES = [(1, 0, 0), (-1, 0, 0)] + [(dx, dy, 0) for dx in (1, -1, 0) for dy in (1, -1)]
ENDS = [(dx, dy, dz) for dx, dy in FLAT[::-1] for dz in (1, -1)]


def act_slope(z):
    e = jnp.exp(-jnp.abs(z))
    q = 1.0 / (1.0 + e)
    sig = jnp.where(z >= 0.0, q, e * q)
    soft = jnp.maximum(z, 0.0) + jnp.log(1.0 + e)
    return NEG * z + (1.0 - NEG) * soft, NEG + (1.0 - NEG) * sig


def dot(a, b):
    return lax.dot_general(a, b, (((1,), (0,)), ((), ())), preferred_element_type=F32)


def dot_nt(a, b):
    return lax.dot_general(a, b, (((1,), (1,)), ((), ())), preferred_element_type=F32)


def roll(v, shift):
    shift = shift % Z
    return v if shift == 0 else pltpu.roll(v, shift, 1)


def lanes(rows):
    return lax.broadcasted_iota(jnp.int32, (rows, Z), 1)


class Level:
    def __init__(self, nx, ny, step):
        self.nx, self.ny, self.step = nx, ny, step
        self.wide = nx + 2

    def at(self, y, x):
        return self.wide * y + x


def put_own(level, v_ref, y, x, pencil):
    v_ref[y + 1, x, C : 2 * C, :] = pencil
    if x + 1 < level.nx:
        v_ref[y + 1, x + 1, 0:C, :] = pencil
    if x >= 1:
        v_ref[y + 1, x - 1, 2 * C : 3 * C, :] = pencil


def spread_y_halo(level, v_ref):
    for y in (0, level.ny + 1):
        for x in range(level.nx):
            if x + 1 < level.nx:
                v_ref[y, x + 1, 0:C, :] = v_ref[y, x, C : 2 * C, :]
            if x >= 1:
                v_ref[y, x - 1, 2 * C : 3 * C, :] = v_ref[y, x, C : 2 * C, :]


def add_face(level, face, y, x, pencil):
    spot = level.at(y + 1, x + 1)
    return jnp.where(lanes(C) // 2 == spot, roll(pencil, 2 * spot + 1), face)


def pack_face(face, z_send):
    odd = lanes(C // 2) % 2 == 1
    top, bottom = face[: C // 2], face[C // 2 :]
    z_send[0] = jnp.where(odd, top, roll(bottom, -1)).astype(BF16)
    z_send[1] = jnp.where(odd, roll(bottom, 1), top).astype(BF16)


def planes(level, z_recv):
    lane = lanes(C // 2)
    spot = lane // 2
    at_y, at_x = spot // level.wide, spot % level.wide

    def side(value, size, d):
        if d == 1:
            return value == 0
        if d == -1:
            return value == size + 1
        return (value >= 1) & (value <= size)

    packed = []
    for which in range(2):
        total = jnp.zeros((C // 2, Z), F32)
        for n, (dx, dy) in enumerate(FLAT):
            shift = -(level.nx * dx) - level.wide * level.ny * dy
            piece = roll(z_recv[n, which].astype(F32), 2 * shift)
            total = jnp.where(side(at_y, level.ny, dy) & side(at_x, level.nx, dx), piece, total)
        packed.append(total)
    low, high = packed
    odd = lane % 2 == 1
    top = jnp.where(odd, roll(low, 1), roll(high, -1))
    bottom = jnp.where(odd, low, high)
    return jnp.concatenate([top, bottom], axis=0)


def halo_columns(level, plane):
    return jnp.concatenate(
        [roll(plane, -2 * (a + level.wide * b)).astype(BF16) for b in range(3) for a in range(3)],
        axis=0,
    )


def stacked(level, v_ref, y):
    return jnp.concatenate(
        [
            jnp.concatenate([v_ref[y + b, x] for x in range(level.nx)], axis=1)
            for b in range(3)
        ],
        axis=0,
    )


def correction(weight, columns):
    p = dot(weight, columns)
    return jnp.where(lanes(C) % 2 == 1, p[:C], p[2 * C :])


def conv_rows(level, weight, v_ref, z_ref):
    lane = lanes(C)
    for y in range(level.ny):
        p = dot(weight, stacked(level, v_ref, y))
        for x in range(level.nx):
            part = p[:, x * Z : (x + 1) * Z]
            left = jnp.where(lane < level.step, 0.0, roll(part[:C], level.step))
            right = jnp.where(lane >= Z - level.step, 0.0, roll(part[2 * C :], -level.step))
            z_ref[y, x] = part[C : 2 * C] + left + right


def fixed(level, fix, z_ref, y, x):
    lane = lanes(C)
    spot = level.at(y, x)
    share = jnp.where(lane == 0, roll(fix, -(2 * spot + 1)), 0.0)
    share = jnp.where(lane == Z - level.step, roll(fix, -level.step - 2 * spot), share)
    return z_ref[y, x] + share


def taps_along_z(level, grad):
    lane = lanes(C)
    first = jnp.where(lane < Z - level.step, roll(grad, -level.step), 0.0)
    last = jnp.where(lane >= level.step, roll(grad, level.step), 0.0)
    return jnp.concatenate([first, grad, last], axis=0).astype(BF16)


def filter_sum(level, g_ref, face, v_ref, columns, total_ref):
    lane = lanes(C)
    own = roll(face, -2 * (level.wide + 1))
    none = jnp.zeros((C, Z), F32)
    edge = jnp.concatenate(
        [jnp.where(lane % 2 == 1, own, 0.0), none, jnp.where(lane % 2 == 0, own, 0.0)], axis=0
    ).astype(BF16)
    total_ref[...] = dot_nt(edge, columns)
    for y in range(level.ny):
        rows = jnp.concatenate([g_ref[y, x] for x in range(level.nx)], axis=1)
        total_ref[...] += dot_nt(rows, stacked(level, v_ref, y))


def kernel(
    sizes,
    field_hbm, cot_hbm, wf_hbm, wd_hbm, wc_hbm, wu_hbm,
    out_ref, a_ref, b_ref,
    field_ref, cot_ref, wf_ref, wd_ref, wc_ref, wu_ref,
    w_ff, w_fb, w_cf, w_cb, w_d, w_dt, w_u,
    v_f, v_c, g_c, g_f,
    zs, zr,
    turn, cot, hid, up_grad, slope_f, slope_d, shifted_f, shifted_c, h_two, g_two, z_f, z_c,
    sum_f, sum_c,
    s_a, s_b, ra_a, ra_b, rb_a, rb_b, rc_a, rc_b,
    local, side_send, side_recv, end_send, end_recv, sum_send, sum_recv,
):
    cx, cy, cz = sizes
    me = (lax.axis_index("gx"), lax.axis_index("gy"), lax.axis_index("gz"))
    fine, coarse = Level(4, 8, 1), Level(2, 4, 2)

    def device(d):
        return tuple(lax.rem(m + (o % n), n) for m, o, n in zip(me, d, sizes))

    def load_in(src, dst, n):
        copy = pltpu.make_async_copy(src, dst, local.at[n])
        copy.start()
        return copy

    field_in = [load_in(field_hbm.at[:, x], field_ref.at[:, x], x) for x in range(4)]
    cot_in = load_in(cot_hbm, cot_ref, 4)
    w_in = [
        load_in(src, dst, 5 + n)
        for n, (src, dst) in enumerate(
            ((wf_hbm, wf_ref), (wu_hbm, wu_ref), (wd_hbm, wd_ref), (wc_hbm, wc_ref))
        )
    ]

    partners = sorted({tuple(o % n for o, n in zip(d, sizes)) for d in SIDES + [(0, 0, 1), (0, 0, -1)]})
    barrier = pltpu.get_barrier_semaphore()
    for d in partners:
        pl.semaphore_signal(barrier, inc=1, device_id=device(d), device_id_type=MESH)

    started = []

    def send(src, dst, send_sem, recv_sem, d):
        copy = pltpu.make_async_remote_copy(
            src_ref=src,
            dst_ref=dst,
            send_sem=send_sem,
            recv_sem=recv_sem,
            device_id=device(d),
            device_id_type=MESH,
        )
        copy.start()
        started.append(copy)
        return copy

    def arrive(copies):
        for copy in copies:
            copy.wait_recv()

    def send_sides(level, which, v_ref, some):
        copies = []
        ny, nx = level.ny, level.nx
        for dx, dy, _ in some:
            n = SIDES.index((dx, dy, 0))
            ys = {0: pl.ds(1, ny), 1: pl.ds(ny, 1), -1: pl.ds(1, 1)}[dy]
            yd = {0: pl.ds(1, ny), 1: pl.ds(0, 1), -1: pl.ds(ny + 1, 1)}[dy]
            xs = {0: pl.ds(0, nx), 1: pl.ds(nx - 1, 1), -1: pl.ds(0, 1)}[dx]
            xd = {0: pl.ds(0, nx), 1: pl.ds(0, 1), -1: pl.ds(nx - 1, 1)}[dx]
            rows = pl.ds({0: C, 1: 0, -1: 2 * C}[dx], C)
            src, dst = v_ref.at[ys, xs, pl.ds(C, C), :], v_ref.at[yd, xd, rows, :]
            copies.append(
                send(src, dst, side_send.at[which, n], side_recv.at[which, n], (dx, dy, 0))
            )
        return copies

    def send_ends(which, some):
        copies = []
        for dx, dy, dz in some:
            n = ENDS.index((dx, dy, dz))
            side = 1 if dz == 1 else 0
            src = zs.at[which, side]
            dst = zr.at[which, FLAT.index((dx, dy)), 1 - side]
            copies.append(send(src, dst, end_send.at[which, n], end_recv.at[which, n], (dx, dy, dz)))
        return copies

    def forward_ends(which):
        copies = []
        for n, (dx, dy) in enumerate(FLAT):
            if n:
                src, dst = zr.at[which, 0], zr.at[which, n]
                copies.append(
                    send(src, dst, end_send.at[which, n], end_recv.at[which, n], (dx, dy, 0))
                )
        return copies

    face = jnp.zeros((C, Z), F32)
    for x in range(4):
        field_in[x].wait()
        turn[x] = field_ref[:, x].astype(F32).reshape(C * 8, Z)
        for y in range(8):
            pencil = turn[x, pl.ds(y, C, stride=8), :]
            put_own(fine, v_f, y, x, pencil.astype(BF16))
            face = add_face(fine, face, y, x, pencil)
    pack_face(face, zs.at[0])

    pl.semaphore_wait(barrier, len(partners))
    ends = send_ends(0, ENDS[-2:])
    sides = send_sides(fine, 0, v_f, SIDES)

    eye = (
        lax.broadcasted_iota(jnp.int32, (C, C), 0) == lax.broadcasted_iota(jnp.int32, (C, C), 1)
    ).astype(BF16)

    def flipped(w):
        return dot_nt(eye, w).astype(BF16)

    def layout_3(w_ref, forward, backward):
        for a in range(3):
            for b in range(3):
                for c in range(3):
                    w = w_ref[a, b, c]
                    m = b * 3 + a
                    forward[c * C : (c + 1) * C, m * C : (m + 1) * C] = w
                    m, k = 8 - m, 2 - c
                    backward[k * C : (k + 1) * C, m * C : (m + 1) * C] = flipped(w)

    for copy in w_in:
        copy.wait()
    layout_3(wf_ref, w_ff, w_fb)
    arrive(ends)
    forwards = forward_ends(0)
    layout_3(wc_ref, w_cf, w_cb)
    for a in range(2):
        for b in range(2):
            for c in range(2):
                m = b * 2 + a
                w = wd_ref[a, b, c]
                w_d[c * C : (c + 1) * C, m * C : (m + 1) * C] = w
                w_dt[m * C : (m + 1) * C, c * C : (c + 1) * C] = flipped(w)
                w_u[c * C : (c + 1) * C, m * C : (m + 1) * C] = flipped(wu_ref[a, b, c])

    def pair(ref, y):
        return jnp.concatenate([ref[y, 0], ref[y, 1]], axis=1)

    arrive(sides)
    spread_y_halo(fine, v_f)
    conv_rows(fine, w_ff[...], v_f, z_f)
    cot_in.wait()
    for x in range(4):
        turn[x] = cot_ref[:, x].astype(F32).reshape(C * 8, Z)
        for y in range(8):
            m = (y % 2) * 2 + x % 2
            pencil = turn[x, pl.ds(y, C, stride=8), :]
            cot[y // 2, x // 2, m * C : (m + 1) * C, :] = pencil.astype(BF16)
    arrive(forwards)
    columns_f = halo_columns(fine, planes(fine, zr.at[0]))
    fix = correction(w_ff[...], columns_f)
    for y in range(8):
        for x in range(4):
            h, s = act_slope(fixed(fine, fix, z_f, y, x))
            m = (y % 2) * 2 + x % 2
            hid[y // 2, x // 2, m * C : (m + 1) * C, :] = h.astype(BF16)
            slope_f[y, x] = s

    even = lanes(C) % 2 == 0
    face = jnp.zeros((C, Z), F32)
    for y in range(4):
        p = dot(w_d[...], pair(hid, y))
        for x in range(2):
            part = p[:, x * Z : (x + 1) * Z]
            d, s = act_slope(part[:C] + roll(part[C:], -1))
            put_own(coarse, v_c, y, x, d.astype(BF16))
            slope_d[y, x] = s
            face = add_face(coarse, face, y, x, jnp.where(even, d, roll(d, 1)))
    pack_face(face, zs.at[1])
    sides = send_sides(coarse, 1, v_c, SIDES[:2])
    ends = send_ends(1, ENDS)
    sides = sides + send_sides(coarse, 1, v_c, SIDES[2:])

    for y in range(4):
        p = dot(w_u[...], pair(cot, y))
        for x in range(2):
            part = p[:, x * Z : (x + 1) * Z]
            up_grad[y, x] = part[:C] + roll(part[C:], -1)

    arrive(sides)
    spread_y_halo(coarse, v_c)
    conv_rows(coarse, w_cf[...], v_c, z_c)
    arrive(ends)
    columns_c = halo_columns(coarse, planes(coarse, zr.at[1]))
    fix = correction(w_cf[...], columns_c)
    face = jnp.zeros((C, Z), F32)
    for y in range(4):
        for x in range(2):
            h, s = act_slope(fixed(coarse, fix, z_c, y, x))
            h = jnp.where(even, h, 0.0)
            h_two[y, x] = jnp.concatenate([h, roll(h, 1)], axis=0).astype(BF16)
            g = jnp.where(even, up_grad[y, x] * s, 0.0).astype(BF16).astype(F32)
            put_own(coarse, g_c, y, x, g.astype(BF16))
            shifted_c[y, x] = taps_along_z(coarse, g)
            face = add_face(coarse, face, y, x, jnp.where(even, g, roll(g, 1)))
    pack_face(face, zs.at[2])
    sides = send_sides(coarse, 2, g_c, SIDES[:2])
    ends = send_ends(2, ENDS)
    sides = sides + send_sides(coarse, 2, g_c, SIDES[2:])

    def long(ref):
        return jnp.concatenate([ref[y, x] for y in range(4) for x in range(2)], axis=1)

    def place(ref, row):
        chunk = ref.shape[1]
        return row // chunk, pl.ds(row % chunk, 16), slice(None)

    def store(ref, block, value):
        for at in range(0, C, 16):
            ref[place(ref, block * C + at)] = value[at : at + 16].astype(BF16)

    def pack_sums(total_ref, ref):
        for c in range(3):
            for q in range(4):
                store(ref, c * 4 + q, total_ref[c * C : (c + 1) * C, q * Z : (q + 1) * Z])
        tail = [total_ref[c * C : (c + 1) * C, 8 * C : 9 * C] for c in range(3)]
        store(ref, 12, jnp.concatenate(tail[:2], axis=1))
        store(ref, 13, jnp.concatenate([tail[2], jnp.zeros((C, C), F32)], axis=1))
        for block in (18, 19):
            store(ref, block, jnp.zeros((C, Z), F32))

    filter_sum(coarse, shifted_c, face, v_c, columns_c, sum_c)
    pack_sums(sum_c, s_a)
    p = dot_nt(long(cot), long(h_two))
    for m in range(4):
        store(s_a, 14 + m, p[m * C : (m + 1) * C])

    in_plane = [(0, j, k) for j in range(cy) for k in range(cz) if (j, k) != (0, 0)]
    in_plane.sort(key=lambda d: -min(d[1], cy - d[1]) - min(d[2], cz - d[2]))
    in_line = sorted([(i, 0, 0) for i in range(1, cx)], key=lambda d: -min(d[0], cx - d[0]))
    plane_at = me[1] * cz + me[2]
    voxels = 4 * 8 * Z * cx * cy * cz
    scale = 1.0 / (voxels**0.5)

    def send_sum(src, dst, stage, which, n, d):
        return send(src, dst, sum_send.at[stage, which, n], sum_recv.at[stage, which, n], d)

    def scatter(which, s, ra):
        out = []
        for n, d in enumerate(in_plane):
            there = device(d)
            out.append(send_sum(s.at[there[1] * cz + there[2]], ra.at[n], 0, which, n, d))
        return out

    def along(which, s, ra, rb, waits):
        arrive(waits)
        total = s[plane_at].astype(F32)
        for n in range(len(in_plane)):
            total = total + ra[n].astype(F32)
        rb[me[0]] = total.astype(BF16)
        return [
            send_sum(rb.at[me[0]], rb.at[me[0]], 1, which, n, d) for n, d in enumerate(in_line)
        ]

    def gather(which, rb, rc, waits):
        arrive(waits)
        total = rb[0].astype(F32)
        for n in range(1, cx):
            total = total + rb[n].astype(F32)
        rc[plane_at] = (total * scale).astype(BF16)
        return [
            send_sum(rc.at[plane_at], rc.at[plane_at], 2, which, n, d)
            for n, d in enumerate(in_plane)
        ]

    waits_a = scatter(0, s_a, ra_a)

    arrive(sides)
    spread_y_halo(coarse, g_c)
    conv_rows(coarse, w_cb[...], g_c, z_c)
    arrive(ends)
    fix = correction(w_cb[...], halo_columns(coarse, planes(coarse, zr.at[2])))
    for y in range(4):
        for x in range(2):
            g = jnp.where(even, fixed(coarse, fix, z_c, y, x) * slope_d[y, x], 0.0)
            g_two[y, x] = jnp.concatenate([g, roll(g, 1)], axis=0).astype(BF16)

    face = jnp.zeros((C, Z), F32)
    for half in range(4):
        p = dot(w_dt[...], pair(g_two, half))
        for b in range(2):
            y = half * 2 + b
            for x in range(4):
                m = b * 2 + x % 2
                wide = p[m * C : (m + 1) * C, (x // 2) * Z : (x // 2 + 1) * Z]
                c = cot[half, x // 2, m * C : (m + 1) * C, :].astype(F32)
                g = ((c + wide) * slope_f[y, x]).astype(BF16).astype(F32)
                put_own(fine, g_f, y, x, g.astype(BF16))
                shifted_f[y, x] = taps_along_z(fine, g)
                face = add_face(fine, face, y, x, g)
    pack_face(face, zs.at[3])
    sides = send_sides(fine, 3, g_f, SIDES)
    ends = send_ends(3, ENDS[-2:])

    p = dot_nt(long(g_two), long(hid))
    for c in range(2):
        for b in range(2):
            store(s_b, 14 + c * 2 + b, p[c * C : (c + 1) * C, b * Z : (b + 1) * Z])
    filter_sum(fine, shifted_f, face, v_f, columns_f, sum_f)
    pack_sums(sum_f, s_b)
    waits_b = scatter(1, s_b, ra_b)

    arrive(ends)
    forwards = forward_ends(3)
    arrive(sides)
    waits_a = along(0, s_a, ra_a, rb_a, waits_a)
    spread_y_halo(fine, g_f)
    conv_rows(fine, w_fb[...], g_f, z_f)
    waits_b = along(1, s_b, ra_b, rb_b, waits_b)
    waits_a = gather(0, rb_a, rc_a, waits_a)
    arrive(forwards)
    fix = correction(w_fb[...], halo_columns(fine, planes(fine, zr.at[3])))
    for x in range(4):
        for y in range(8):
            turn[x, pl.ds(y, C, stride=8), :] = fixed(fine, fix, z_f, y, x)
        out_ref[:, x] = turn[x].reshape(C, 8, Z).astype(BF16)
    waits_b = gather(1, rb_b, rc_b, waits_b)
    arrive(waits_a)
    a_ref[...] = rc_a[...]
    arrive(waits_b)
    b_ref[...] = rc_b[...]
    for copy in started:
        copy.wait_send()


def finish(
    field_ref, a_ref, b_ref,
    out_hbm, of_hbm, od_hbm, oc_hbm, ou_hbm,
    of_ref, od_ref, oc_ref, ou_ref,
    sems,
):
    copies = []

    def write(src, dst):
        copy = pltpu.make_async_copy(src, dst, sems.at[len(copies)])
        copy.start()
        copies.append(copy)

    write(field_ref, out_hbm)

    def load(ref, block):
        rows = []
        for at in range(block * C, (block + 1) * C, 16):
            rows.append(ref[at // ref.shape[1], pl.ds(at % ref.shape[1], 16), :])
        return jnp.concatenate(rows, axis=0).astype(F32)

    def unpack_sums(ref, o_ref):
        for block in range(14):
            value = load(ref, block)
            for half in range(2):
                if block < 12:
                    c, m = block // 4, (block % 4) * 2 + half
                else:
                    c, m = (block - 12) * 2 + half, 8
                if c < 3:
                    o_ref[m % 3, m // 3, c] = value[:, half * C : (half + 1) * C]

    unpack_sums(a_ref, oc_ref)
    write(oc_ref, oc_hbm)
    unpack_sums(b_ref, of_ref)
    write(of_ref, of_hbm)
    for m in range(4):
        value = load(a_ref, 14 + m)
        for c in range(2):
            ou_ref[m % 2, m // 2, c] = value[:, c * C : (c + 1) * C]
    write(ou_ref, ou_hbm)
    for c in range(2):
        for b in range(2):
            value = load(b_ref, 14 + c * 2 + b)
            for a in range(2):
                od_ref[a, b, c] = value[:, a * C : (a + 1) * C]
    write(od_ref, od_hbm)
    for copy in copies:
        copy.wait()


def solution(mesh):
    sizes = (mesh.shape["gx"], mesh.shape["gy"], mesh.shape["gz"])
    cx, cy, cz = sizes
    plane = cy * cz
    rows = 20 * C // plane

    def step(field, cotangent, w_fine, w_down, w_coarse, w_up):
        vmem = pl.BlockSpec(memory_space=pltpu.VMEM)
        hbm = pl.BlockSpec(memory_space=pltpu.HBM)
        three, two = (3, 3, 3, C, C), (2, 2, 2, C, C)
        packed = jax.ShapeDtypeStruct((plane, rows, Z), BF16)
        whole = jax.ShapeDtypeStruct((C, 4, 8, Z), BF16)
        inputs = [
            pltpu.with_memory_space_constraint(v, pltpu.HBM)
            for v in (field, cotangent, w_fine, w_down, w_coarse, w_up)
        ]
        grad, sums_a, sums_b = pl.pallas_call(
            functools.partial(kernel, sizes),
            out_shape=[whole, packed, packed],
            in_specs=[hbm] * 6,
            out_specs=[vmem] * 3,
            scratch_shapes=[
                pltpu.VMEM((C, 4, 8, Z), BF16),
                pltpu.VMEM((C, 4, 8, Z), BF16),
                pltpu.VMEM(three, BF16),
                pltpu.VMEM(two, BF16),
                pltpu.VMEM(three, BF16),
                pltpu.VMEM(two, BF16),
                pltpu.VMEM((3 * C, 9 * C), BF16),
                pltpu.VMEM((3 * C, 9 * C), BF16),
                pltpu.VMEM((3 * C, 9 * C), BF16),
                pltpu.VMEM((3 * C, 9 * C), BF16),
                pltpu.VMEM((2 * C, 4 * C), BF16),
                pltpu.VMEM((4 * C, 2 * C), BF16),
                pltpu.VMEM((2 * C, 4 * C), BF16),
                pltpu.VMEM((10, 4, 3 * C, Z), BF16),
                pltpu.VMEM((6, 2, 3 * C, Z), BF16),
                pltpu.VMEM((6, 2, 3 * C, Z), BF16),
                pltpu.VMEM((10, 4, 3 * C, Z), BF16),
                pltpu.VMEM((4, 2, C // 2, Z), BF16),
                pltpu.VMEM((4, 9, 2, C // 2, Z), BF16),
                pltpu.VMEM((4, 8 * C, Z), F32),
                pltpu.VMEM((4, 2, 4 * C, Z), BF16),
                pltpu.VMEM((4, 2, 4 * C, Z), BF16),
                pltpu.VMEM((4, 2, C, Z), F32),
                pltpu.VMEM((8, 4, C, Z), F32),
                pltpu.VMEM((4, 2, C, Z), F32),
                pltpu.VMEM((8, 4, 3 * C, Z), BF16),
                pltpu.VMEM((4, 2, 3 * C, Z), BF16),
                pltpu.VMEM((4, 2, 2 * C, Z), BF16),
                pltpu.VMEM((4, 2, 2 * C, Z), BF16),
                pltpu.VMEM((8, 4, C, Z), F32),
                pltpu.VMEM((4, 2, C, Z), F32),
                pltpu.VMEM((3 * C, 9 * C), F32),
                pltpu.VMEM((3 * C, 9 * C), F32),
                pltpu.VMEM((plane, rows, Z), BF16),
                pltpu.VMEM((plane, rows, Z), BF16),
                pltpu.VMEM((plane - 1, rows, Z), BF16),
                pltpu.VMEM((plane - 1, rows, Z), BF16),
                pltpu.VMEM((cx, rows, Z), BF16),
                pltpu.VMEM((cx, rows, Z), BF16),
                pltpu.VMEM((plane, rows, Z), BF16),
                pltpu.VMEM((plane, rows, Z), BF16),
                pltpu.SemaphoreType.DMA((9,)),
                pltpu.SemaphoreType.DMA((4, 8)),
                pltpu.SemaphoreType.DMA((4, 8)),
                pltpu.SemaphoreType.DMA((4, 18)),
                pltpu.SemaphoreType.DMA((4, 18)),
                pltpu.SemaphoreType.DMA((3, 2, 15)),
                pltpu.SemaphoreType.DMA((3, 2, 15)),
            ],
            compiler_params=pltpu.CompilerParams(
                collective_id=0, has_side_effects=True, vmem_limit_bytes=48 * 1024 * 1024
            ),
        )(*inputs)
        return pl.pallas_call(
            finish,
            out_shape=[whole]
            + [jax.ShapeDtypeStruct(s, F32) for s in (three, two, three, two)],
            in_specs=[vmem] * 3,
            out_specs=[hbm] * 5,
            scratch_shapes=[pltpu.VMEM(s, F32) for s in (three, two, three, two)]
            + [pltpu.SemaphoreType.DMA((5,))],
            compiler_params=pltpu.CompilerParams(vmem_limit_bytes=32 * 1024 * 1024),
        )(grad, sums_a, sums_b)

    return jax.shard_map(
        step,
        mesh=mesh,
        in_specs=(P(None, "gx", "gy", "gz"), P(None, "gx", "gy", "gz"), P(), P(), P(), P()),
        out_specs=(P(None, "gx", "gy", "gz"), P(), P(), P(), P()),
        check_vma=False,
    )
```

```python
import functools

import jax
import jax.numpy as jnp
from jax import lax
from jax.experimental import pallas as pl
from jax.experimental.pallas import tpu as pltpu
from jax.sharding import PartitionSpec as P

MESH = pl.DeviceIdType.MESH
F32 = jnp.float32
BF16 = jnp.bfloat16
C = 64
Z = 128
NEG = 0.2

FLAT = [(dx, dy) for dx in (0, 1, -1) for dy in (0, 1, -1)]

SIDES = [(1, 0, 0), (-1, 0, 0)] + [(dx, dy, 0) for dx in (1, -1, 0) for dy in (1, -1)]
ENDS = [(dx, dy, dz) for dx, dy in FLAT[::-1] for dz in (1, -1)]


def act_slope(z):
    e = jnp.exp(-jnp.abs(z))
    q = 1.0 / (1.0 + e)
    sig = jnp.where(z >= 0.0, q, e * q)
    soft = jnp.maximum(z, 0.0) + jnp.log(1.0 + e)
    return NEG * z + (1.0 - NEG) * soft, NEG + (1.0 - NEG) * sig


def dot(a, b):
    return lax.dot_general(a, b, (((1,), (0,)), ((), ())), preferred_element_type=F32)


def dot_nt(a, b):
    return lax.dot_general(a, b, (((1,), (1,)), ((), ())), preferred_element_type=F32)


def roll(v, shift):
    shift = shift % Z
    return v if shift == 0 else pltpu.roll(v, shift, 1)


def lanes(rows):
    return lax.broadcasted_iota(jnp.int32, (rows, Z), 1)


class Level:
    def __init__(self, nx, ny, step, wide):
        self.nx, self.ny, self.step = nx, ny, step
        self.wide = wide

    def at(self, y, x):
        return self.wide * y + x


def put_own(level, v_ref, y, x, pencil):
    v_ref[y + 1, x, C : 2 * C, :] = pencil
    if x + 1 < level.nx:
        v_ref[y + 1, x + 1, 0:C, :] = pencil
    if x >= 1:
        v_ref[y + 1, x - 1, 2 * C : 3 * C, :] = pencil


def spread_y_halo(level, v_ref):
    for y in (0, level.ny + 1):
        for x in range(level.nx):
            if x + 1 < level.nx:
                v_ref[y, x + 1, 0:C, :] = v_ref[y, x, C : 2 * C, :]
            if x >= 1:
                v_ref[y, x - 1, 2 * C : 3 * C, :] = v_ref[y, x, C : 2 * C, :]


def add_face(level, face, y, x, pencil):
    spot = level.at(y + 1, x + 1)
    return jnp.where(lanes(C) // 2 == spot, roll(pencil, 2 * spot + 1), face)


def pack_face(face, z_send):
    odd = lanes(C // 2) % 2 == 1
    top, bottom = face[: C // 2], face[C // 2 :]
    z_send[0] = jnp.where(odd, top, roll(bottom, -1)).astype(BF16)
    z_send[1] = jnp.where(odd, roll(bottom, 1), top).astype(BF16)


def planes(level, z_recv):
    lane = lanes(C // 2)
    spot = lane // 2
    at_y, at_x = spot // level.wide, spot % level.wide

    def side(value, size, d):
        if d == 1:
            return value == 0
        if d == -1:
            return value == size + 1
        return (value >= 1) & (value <= size)

    packed = []
    for which in range(2):
        total = jnp.zeros((C // 2, Z), F32)
        for n, (dx, dy) in enumerate(FLAT):
            shift = -(level.nx * dx) - level.wide * level.ny * dy
            piece = roll(z_recv[n, which].astype(F32), 2 * shift)
            total = jnp.where(side(at_y, level.ny, dy) & side(at_x, level.nx, dx), piece, total)
        packed.append(total)
    low, high = packed
    odd = lane % 2 == 1
    top = jnp.where(odd, roll(low, 1), roll(high, -1))
    bottom = jnp.where(odd, low, high)
    return jnp.concatenate([top, bottom], axis=0)


def pack_ends(near, far, z_send):
    odd = lanes(C) % 2 == 1
    left = lanes(C // 2) < C
    down = jnp.where(odd, far, roll(near, -1))
    up = jnp.where(odd, roll(far, 1), near)
    for n, value in enumerate((down, up)):
        packed = jnp.where(left, value[: C // 2], roll(value[C // 2 :], C))
        z_send[n] = packed.astype(BF16)


def outer_planes(z_recv):
    lane = lanes(C)
    spot = lane // 2
    at_y, at_x = spot // 6, spot % 6
    sides = []
    for which in range(2):
        total = jnp.zeros((C, Z), F32)
        for n, (dx, dy) in enumerate(FLAT):
            first_y, last_y = {0: (2, 5), 1: (0, 1), -1: (6, 7)}[dy]
            first_x = 2 - 2 * dx
            mine = (at_y >= first_y) & (at_y <= last_y) & (at_x >= first_x) & (at_x <= first_x + 1)
            packed = z_recv[n, which].astype(F32)
            value = jnp.concatenate([packed, roll(packed, C)], axis=0)
            total = jnp.where(mine, roll(value, 2 * (14 - 2 * dx - 24 * dy)), total)
        sides.append(total)
    low, high = sides
    odd = lane % 2 == 1
    return jnp.where(odd, roll(low, 1), high), jnp.where(odd, low, roll(high, -1))


def halo_columns(level, plane):
    return jnp.concatenate(
        [roll(plane, -2 * (a + level.wide * b)).astype(BF16) for b in range(3) for a in range(3)],
        axis=0,
    )


def stacked(level, v_ref, y):
    return jnp.concatenate(
        [
            jnp.concatenate([v_ref[y + b, x] for x in range(level.nx)], axis=1)
            for b in range(3)
        ],
        axis=0,
    )


def correction(weight, columns):
    p = dot(weight, columns)
    return jnp.where(lanes(C) % 2 == 1, p[:C], p[2 * C :])


def conv_rows(level, weight, v_ref, z_ref, beyond=None):
    lane = lanes(C)
    for y in range(level.ny):
        p = dot(weight, stacked(level, v_ref, y))
        for x in range(level.nx):
            part = p[:, x * Z : (x + 1) * Z]
            left = jnp.where(lane < level.step, 0.0, roll(part[:C], level.step))
            right = jnp.where(lane >= Z - level.step, 0.0, roll(part[2 * C :], -level.step))
            z_ref[y, x] = part[C : 2 * C] + left + right
            if beyond is not None:
                spot = level.at(y, x)
                low = roll(part[2 * C :], 2 * spot + 1)
                high = roll(part[:C], 2 * spot - Z + level.step)
                beyond = jnp.where(lane == 2 * spot + 1, low, beyond)
                beyond = jnp.where(lane == 2 * spot, high, beyond)
    return beyond


def fixed(level, fix, z_ref, y, x):
    lane = lanes(C)
    spot = level.at(y, x)
    share = jnp.where(lane == 0, roll(fix, -(2 * spot + 1)), 0.0)
    share = jnp.where(lane == Z - level.step, roll(fix, -level.step - 2 * spot), share)
    return z_ref[y, x] + share


def taps_along_z(level, grad):
    lane = lanes(C)
    first = jnp.where(lane < Z - level.step, roll(grad, -level.step), 0.0)
    last = jnp.where(lane >= level.step, roll(grad, level.step), 0.0)
    return jnp.concatenate([first, grad, last], axis=0).astype(BF16)


def filter_sum(level, g_ref, face, v_ref, columns, total_ref):
    lane = lanes(C)
    own = roll(face, -2 * (level.wide + 1))
    none = jnp.zeros((C, Z), F32)
    edge = jnp.concatenate(
        [jnp.where(lane % 2 == 1, own, 0.0), none, jnp.where(lane % 2 == 0, own, 0.0)], axis=0
    ).astype(BF16)
    total_ref[...] = dot_nt(edge, columns)
    for y in range(level.ny):
        rows = jnp.concatenate([g_ref[y, x] for x in range(level.nx)], axis=1)
        total_ref[...] += dot_nt(rows, stacked(level, v_ref, y))


def kernel(
    sizes,
    field_hbm, cot_hbm, wf_hbm, wd_hbm, wc_hbm, wu_hbm,
    out_ref, a_ref, b_ref,
    field_ref, cot_ref, wf_ref, wd_ref, wc_ref, wu_ref,
    w_ff, w_fb, w_cf, w_cb, w_d, w_dt, w_u,
    v_f, v_e, g_c, g_f, both, up_ext,
    zs, zr,
    turn, cot, hid, up_grad, slope_f, slope_d, shifted_f, shifted_c, h_two, g_two, z_f, z_c, z_e,
    sum_f, sum_c,
    s_a, s_b, ra_a, ra_b, rb_a, rb_b, rc_a, rc_b,
    local, side_send, side_recv, end_send, end_recv, sum_send, sum_recv,
):
    cx, cy, cz = sizes
    me = (lax.axis_index("gx"), lax.axis_index("gy"), lax.axis_index("gz"))
    fine, coarse, outer = Level(4, 8, 1, 6), Level(2, 4, 2, 6), Level(4, 6, 2, 6)

    def device(d):
        return tuple(lax.rem(m + (o % n), n) for m, o, n in zip(me, d, sizes))

    first = SIDES + [(0, 0, 1), (0, 0, -1)] + [(i, 0, 0) for i in range(3, cx - 2)]
    partners = sorted({tuple(o % n for o, n in zip(d, sizes)) for d in first})
    barrier = pltpu.get_barrier_semaphore()
    for d in partners:
        pl.semaphore_signal(barrier, inc=1, device_id=device(d), device_id_type=MESH)

    def load_in(src, dst, n):
        copy = pltpu.make_async_copy(src, dst, local.at[n])
        copy.start()
        return copy

    field_in = [load_in(field_hbm.at[:, x], field_ref.at[:, x], x) for x in range(4)]
    cot_in = load_in(cot_hbm, cot_ref, 4)
    w_in = [
        load_in(src, dst, 5 + n)
        for n, (src, dst) in enumerate(
            ((wf_hbm, wf_ref), (wu_hbm, wu_ref), (wd_hbm, wd_ref), (wc_hbm, wc_ref))
        )
    ]

    started = []

    def send(src, dst, send_sem, recv_sem, d):
        copy = pltpu.make_async_remote_copy(
            src_ref=src,
            dst_ref=dst,
            send_sem=send_sem,
            recv_sem=recv_sem,
            device_id=device(d),
            device_id_type=MESH,
        )
        copy.start()
        started.append(copy)
        return copy

    def arrive(copies):
        for copy in copies:
            copy.wait_recv()

    def send_sides(which, views):
        copies = []
        for n, (dx, dy, _) in enumerate(SIDES):
            src, dst = views(dx, dy)
            copies.append(
                send(src, dst, side_send.at[which, n], side_recv.at[which, n], (dx, dy, 0))
            )
        return copies

    def along_axis(size, depth, d):
        src = {0: pl.ds(depth, size), 1: pl.ds(size, depth), -1: pl.ds(depth, depth)}[d]
        dst = {0: pl.ds(depth, size), 1: pl.ds(0, depth), -1: pl.ds(size + depth, depth)}[d]
        return src, dst

    def fine_views(v_ref):
        def views(dx, dy):
            ys, yd = along_axis(8, 1, dy)
            xs = {0: pl.ds(0, 4), 1: pl.ds(3, 1), -1: pl.ds(0, 1)}[dx]
            xd = {0: pl.ds(0, 4), 1: pl.ds(0, 1), -1: pl.ds(3, 1)}[dx]
            rows = pl.ds({0: C, 1: 0, -1: 2 * C}[dx], C)
            return v_ref.at[ys, xs, pl.ds(C, C), :], v_ref.at[yd, xd, rows, :]

        return views

    def up_views(dx, dy):
        (ys, yd), (xs, xd) = along_axis(4, 1, dy), along_axis(2, 1, dx)
        return up_ext.at[ys, xs], up_ext.at[yd, xd]

    def down_views(dx, dy):
        ys, yd = along_axis(4, 2, dy)
        return both.at[ys, 1], both.at[yd, 1 - dx]

    def send_ends(which, some):
        copies = []
        for dx, dy, dz in some:
            n = ENDS.index((dx, dy, dz))
            side = 1 if dz == 1 else 0
            src = zs.at[which, side]
            dst = zr.at[which, FLAT.index((dx, dy)), 1 - side]
            copies.append(send(src, dst, end_send.at[which, n], end_recv.at[which, n], (dx, dy, dz)))
        return copies

    def forward_ends(which):
        copies = []
        for n, (dx, dy) in enumerate(FLAT):
            if n:
                src, dst = zr.at[which, 0], zr.at[which, n]
                copies.append(
                    send(src, dst, end_send.at[which, n], end_recv.at[which, n], (dx, dy, 0))
                )
        return copies

    face = jnp.zeros((C, Z), F32)
    for x in range(4):
        field_in[x].wait()
        turn[x] = field_ref[:, x].astype(F32).reshape(C * 8, Z)
        for y in range(8):
            pencil = turn[x, pl.ds(y, C, stride=8), :]
            put_own(fine, v_f, y, x, pencil.astype(BF16))
            face = add_face(fine, face, y, x, pencil)
    pack_face(face, zs.at[0])

    pl.semaphore_wait(barrier, len(partners))
    ends = send_ends(0, ENDS[-2:])
    sides = send_sides(0, fine_views(v_f))

    eye = (
        lax.broadcasted_iota(jnp.int32, (C, C), 0) == lax.broadcasted_iota(jnp.int32, (C, C), 1)
    ).astype(BF16)

    def flipped(w):
        return dot_nt(eye, w).astype(BF16)

    def layout_3(w_ref, forward, backward):
        for a in range(3):
            for b in range(3):
                for c in range(3):
                    w = w_ref[a, b, c]
                    m = b * 3 + a
                    forward[c * C : (c + 1) * C, m * C : (m + 1) * C] = w
                    m, k = 8 - m, 2 - c
                    backward[k * C : (k + 1) * C, m * C : (m + 1) * C] = flipped(w)

    for copy in w_in:
        copy.wait()
    layout_3(wf_ref, w_ff, w_fb)
    arrive(ends)
    forwards = forward_ends(0)
    layout_3(wc_ref, w_cf, w_cb)
    for a in range(2):
        for b in range(2):
            for c in range(2):
                m = b * 2 + a
                w = wd_ref[a, b, c]
                w_d[c * C : (c + 1) * C, m * C : (m + 1) * C] = w
                w_dt[m * C : (m + 1) * C, c * C : (c + 1) * C] = flipped(w)
                w_u[c * C : (c + 1) * C, m * C : (m + 1) * C] = flipped(wu_ref[a, b, c])

    def pair(ref, y):
        return jnp.concatenate([ref[y, 0], ref[y, 1]], axis=1)

    cot_in.wait()
    for x in range(4):
        turn[x] = cot_ref[:, x].astype(F32).reshape(C * 8, Z)
        for y in range(8):
            m = (y % 2) * 2 + x % 2
            pencil = turn[x, pl.ds(y, C, stride=8), :]
            cot[y // 2, x // 2, m * C : (m + 1) * C, :] = pencil.astype(BF16)
    even = lanes(C) % 2 == 0
    odd = lanes(C) % 2 == 1
    face = jnp.zeros((C, Z), F32)
    for y in range(4):
        p = dot(w_u[...], pair(cot, y))
        for x in range(2):
            part = p[:, x * Z : (x + 1) * Z]
            g = part[:C] + roll(part[C:], -1)
            up_grad[y, x] = g
            up_ext[y + 1, x + 1] = g.astype(BF16)
            face = add_face(coarse, face, y, x, jnp.where(even, g, roll(g, 1)))
    pack_face(face, zs.at[1])

    arrive(sides)
    spread_y_halo(fine, v_f)
    conv_rows(fine, w_ff[...], v_f, z_f)
    up_ends = send_ends(1, ENDS[-2:])
    up_sides = send_sides(1, up_views)
    arrive(forwards)
    columns_f = halo_columns(fine, planes(fine, zr.at[0]))
    fix = correction(w_ff[...], columns_f)
    for y in range(8):
        for x in range(4):
            h, s = act_slope(fixed(fine, fix, z_f, y, x))
            m = (y % 2) * 2 + x % 2
            hid[y // 2, x // 2, m * C : (m + 1) * C, :] = h.astype(BF16)
            slope_f[y, x] = s

    lane = lanes(C)
    near = jnp.zeros((C, Z), F32)
    far = jnp.zeros((C, Z), F32)
    for y in range(4):
        p = dot(w_d[...], pair(hid, y))
        row = []
        for x in range(2):
            part = p[:, x * Z : (x + 1) * Z]
            d, s = act_slope(part[:C] + roll(part[C:], -1))
            slope_d[y, x] = s
            row.append(d)
            spot = coarse.at(y, x)
            near = jnp.where(
                lane // 2 == spot, roll(jnp.where(even, d, roll(d, 1)), 2 * spot + 1), near
            )
            far = jnp.where(lane == 2 * spot + 1, roll(d, 2 * spot - 1), far)
            far = jnp.where(lane == 2 * spot, roll(d, 2 * spot - 124), far)
        both[y + 2, 1] = jnp.where(even, row[0], roll(row[1], 1)).astype(BF16)
    pack_ends(near, far, zs.at[2])
    ends = send_ends(2, ENDS)
    sides = send_sides(2, down_views)

    arrive(up_ends)
    forwards = forward_ends(1)

    def unpack(y, block):
        value = both[y, block]
        moved = roll(value.astype(F32), -1).astype(BF16)
        for x, pencil in ((2 * block, value), (2 * block + 1, moved)):
            for a in range(3):
                if 0 <= x - a < 4:
                    v_e[y, x - a, a * C : (a + 1) * C, :] = pencil

    for y in range(4):
        unpack(y + 2, 1)
    arrive(sides)
    for y in range(8):
        for block in range(3):
            if block != 1 or not 2 <= y < 6:
                unpack(y, block)
    beyond = conv_rows(outer, w_cf[...], v_e, z_e, jnp.zeros((C, Z), F32))
    arrive(ends)
    plane_1, plane_2 = outer_planes(zr.at[2])
    p_1 = dot(w_cf[...], halo_columns(outer, plane_1))
    p_2 = dot(w_cf[...], halo_columns(outer, plane_2))
    columns_c = halo_columns(outer, roll(plane_1, -14))
    fix = jnp.where(odd, p_1[:C], p_1[2 * C :])
    beyond = beyond + p_1[C : 2 * C] + jnp.where(odd, p_2[:C], p_2[2 * C :])
    arrive(up_sides)
    face = jnp.zeros((C, Z), F32)
    for y in range(6):
        for x in range(4):
            h, s = act_slope(fixed(outer, fix, z_e, y, x))
            own = 1 <= y < 5 and 1 <= x < 3
            up = up_grad[y - 1, x - 1] if own else up_ext[y, x].astype(F32)
            g = jnp.where(even, up * s, 0.0).astype(BF16).astype(F32)
            for a in range(3):
                if 0 <= x - a < 2:
                    g_c[y, x - a, a * C : (a + 1) * C, :] = g.astype(BF16)
            if own:
                h = jnp.where(even, h, 0.0)
                h_two[y - 1, x - 1] = jnp.concatenate([h, roll(h, 1)], axis=0).astype(BF16)
                shifted_c[y - 1, x - 1] = taps_along_z(coarse, g)
                face = add_face(coarse, face, y - 1, x - 1, jnp.where(even, g, roll(g, 1)))
    arrive(forwards)
    g_plane = planes(coarse, zr.at[1]) * act_slope(beyond)[1]
    g_plane = g_plane.astype(BF16).astype(F32)

    def long(ref):
        return jnp.concatenate([ref[y, x] for y in range(4) for x in range(2)], axis=1)

    def place(ref, row):
        chunk = ref.shape[1]
        return row // chunk, pl.ds(row % chunk, 16), slice(None)

    def store(ref, block, value):
        for at in range(0, C, 16):
            ref[place(ref, block * C + at)] = value[at : at + 16].astype(BF16)

    def pack_sums(total_ref, ref):
        for c in range(3):
            for q in range(4):
                store(ref, c * 4 + q, total_ref[c * C : (c + 1) * C, q * Z : (q + 1) * Z])
        tail = [total_ref[c * C : (c + 1) * C, 8 * C : 9 * C] for c in range(3)]
        store(ref, 12, jnp.concatenate(tail[:2], axis=1))
        store(ref, 13, jnp.concatenate([tail[2], jnp.zeros((C, C), F32)], axis=1))
    in_plane = [(0, j, k) for j in range(cy) for k in range(cz) if (j, k) != (0, 0)]
    in_plane.sort(key=lambda d: -min(d[1], cy - d[1]) - min(d[2], cz - d[2]))
    in_line = sorted([(i, 0, 0) for i in range(1, cx)], key=lambda d: -min(d[0], cx - d[0]))
    plane_at = me[1] * cz + me[2]
    voxels = 4 * 8 * Z * cx * cy * cz
    scale = 1.0 / (voxels**0.5)

    def send_sum(src, dst, stage, which, n, d):
        return send(src, dst, sum_send.at[stage, which, n], sum_recv.at[stage, which, n], d)

    def scatter(which, s, ra):
        out = []
        for n, d in enumerate(in_plane):
            there = device(d)
            out.append(send_sum(s.at[there[1] * cz + there[2]], ra.at[n], 0, which, n, d))
        return out

    def along(which, s, ra, rb, waits):
        arrive(waits)
        total = s[plane_at].astype(F32)
        for n in range(len(in_plane)):
            total = total + ra[n].astype(F32)
        rb[me[0]] = total.astype(BF16)
        return [
            send_sum(rb.at[me[0]], rb.at[me[0]], 1, which, n, d) for n, d in enumerate(in_line)
        ]

    def gather(which, rb, rc, waits):
        arrive(waits)
        total = rb[0].astype(F32)
        for n in range(1, cx):
            total = total + rb[n].astype(F32)
        rc[plane_at] = (total * scale).astype(BF16)
        return [
            send_sum(rc.at[plane_at], rc.at[plane_at], 2, which, n, d)
            for n, d in enumerate(in_plane)
        ]

    conv_rows(coarse, w_cb[...], g_c, z_c)
    fix = correction(w_cb[...], halo_columns(coarse, g_plane))
    for y in range(4):
        for x in range(2):
            g = jnp.where(even, fixed(coarse, fix, z_c, y, x) * slope_d[y, x], 0.0)
            g_two[y, x] = jnp.concatenate([g, roll(g, 1)], axis=0).astype(BF16)

    filter_sum(coarse, shifted_c, face, v_e.at[pl.ds(1, 6), pl.ds(1, 2)], columns_c, sum_c)
    pack_sums(sum_c, s_a)
    p = dot_nt(long(cot), long(h_two))
    for m in range(4):
        store(s_a, 14 + m, p[m * C : (m + 1) * C])
    p = dot_nt(long(g_two), long(hid))
    for c in range(2):
        for b in range(2):
            store(s_a, 18 + c * 2 + b, p[c * C : (c + 1) * C, b * Z : (b + 1) * Z])
    for block in (22, 23):
        store(s_a, block, jnp.zeros((C, Z), F32))
    waits_a = scatter(0, s_a, ra_a)

    face = jnp.zeros((C, Z), F32)
    for half in range(4):
        p = dot(w_dt[...], pair(g_two, half))
        for b in range(2):
            y = half * 2 + b
            for x in range(4):
                m = b * 2 + x % 2
                wide = p[m * C : (m + 1) * C, (x // 2) * Z : (x // 2 + 1) * Z]
                c = cot[half, x // 2, m * C : (m + 1) * C, :].astype(F32)
                g = ((c + wide) * slope_f[y, x]).astype(BF16).astype(F32)
                put_own(fine, g_f, y, x, g.astype(BF16))
                shifted_f[y, x] = taps_along_z(fine, g)
                face = add_face(fine, face, y, x, g)
    pack_face(face, zs.at[3])

    filter_sum(fine, shifted_f, face, v_f, columns_f, sum_f)
    pack_sums(sum_f, s_b)
    for block in (14, 15):
        store(s_b, block, jnp.zeros((C, Z), F32))
    waits_b = scatter(1, s_b, ra_b)
    ends = send_ends(3, ENDS[-2:])
    sides = send_sides(3, fine_views(g_f))

    waits_a = along(0, s_a, ra_a, rb_a, waits_a)
    waits_b = along(1, s_b, ra_b, rb_b, waits_b)
    arrive(ends)
    forwards = forward_ends(3)
    arrive(sides)
    spread_y_halo(fine, g_f)
    conv_rows(fine, w_fb[...], g_f, z_f)
    waits_a = gather(0, rb_a, rc_a, waits_a)
    waits_b = gather(1, rb_b, rc_b, waits_b)
    arrive(forwards)
    fix = correction(w_fb[...], halo_columns(fine, planes(fine, zr.at[3])))
    for x in range(4):
        for y in range(8):
            turn[x, pl.ds(y, C, stride=8), :] = fixed(fine, fix, z_f, y, x)
        out_ref[:, x] = turn[x].reshape(C, 8, Z).astype(BF16)
    arrive(waits_a)
    a_ref[...] = rc_a[...]
    arrive(waits_b)
    b_ref[...] = rc_b[...]
    for copy in started:
        copy.wait_send()


def finish(
    field_ref, a_ref, b_ref,
    out_hbm, of_hbm, od_hbm, oc_hbm, ou_hbm,
    of_ref, od_ref, oc_ref, ou_ref,
    sems,
):
    copies = []

    def write(src, dst):
        copy = pltpu.make_async_copy(src, dst, sems.at[len(copies)])
        copy.start()
        copies.append(copy)

    write(field_ref, out_hbm)

    def load(ref, block):
        rows = []
        for at in range(block * C, (block + 1) * C, 16):
            rows.append(ref[at // ref.shape[1], pl.ds(at % ref.shape[1], 16), :])
        return jnp.concatenate(rows, axis=0).astype(F32)

    def unpack_sums(ref, o_ref):
        for block in range(14):
            value = load(ref, block)
            for half in range(2):
                if block < 12:
                    c, m = block // 4, (block % 4) * 2 + half
                else:
                    c, m = (block - 12) * 2 + half, 8
                if c < 3:
                    o_ref[m % 3, m // 3, c] = value[:, half * C : (half + 1) * C]

    unpack_sums(a_ref, oc_ref)
    write(oc_ref, oc_hbm)
    unpack_sums(b_ref, of_ref)
    write(of_ref, of_hbm)
    for m in range(4):
        value = load(a_ref, 14 + m)
        for c in range(2):
            ou_ref[m % 2, m // 2, c] = value[:, c * C : (c + 1) * C]
    write(ou_ref, ou_hbm)
    for c in range(2):
        for b in range(2):
            value = load(a_ref, 18 + c * 2 + b)
            for a in range(2):
                od_ref[a, b, c] = value[:, a * C : (a + 1) * C]
    write(od_ref, od_hbm)
    for copy in copies:
        copy.wait()


def solution(mesh):
    sizes = (mesh.shape["gx"], mesh.shape["gy"], mesh.shape["gz"])
    cx, cy, cz = sizes
    plane = cy * cz
    rows_a, rows_b = 24 * C // plane, 16 * C // plane

    def step(field, cotangent, w_fine, w_down, w_coarse, w_up):
        vmem = pl.BlockSpec(memory_space=pltpu.VMEM)
        hbm = pl.BlockSpec(memory_space=pltpu.HBM)
        three, two = (3, 3, 3, C, C), (2, 2, 2, C, C)
        packed = [jax.ShapeDtypeStruct((plane, rows, Z), BF16) for rows in (rows_a, rows_b)]
        whole = jax.ShapeDtypeStruct((C, 4, 8, Z), BF16)
        inputs = [
            pltpu.with_memory_space_constraint(v, pltpu.HBM)
            for v in (field, cotangent, w_fine, w_down, w_coarse, w_up)
        ]
        grad, sums_a, sums_b = pl.pallas_call(
            functools.partial(kernel, sizes),
            out_shape=[whole, *packed],
            in_specs=[hbm] * 6,
            out_specs=[vmem] * 3,
            scratch_shapes=[
                pltpu.VMEM((C, 4, 8, Z), BF16),
                pltpu.VMEM((C, 4, 8, Z), BF16),
                pltpu.VMEM(three, BF16),
                pltpu.VMEM(two, BF16),
                pltpu.VMEM(three, BF16),
                pltpu.VMEM(two, BF16),
                pltpu.VMEM((3 * C, 9 * C), BF16),
                pltpu.VMEM((3 * C, 9 * C), BF16),
                pltpu.VMEM((3 * C, 9 * C), BF16),
                pltpu.VMEM((3 * C, 9 * C), BF16),
                pltpu.VMEM((2 * C, 4 * C), BF16),
                pltpu.VMEM((4 * C, 2 * C), BF16),
                pltpu.VMEM((2 * C, 4 * C), BF16),
                pltpu.VMEM((10, 4, 3 * C, Z), BF16),
                pltpu.VMEM((8, 4, 3 * C, Z), BF16),
                pltpu.VMEM((6, 2, 3 * C, Z), BF16),
                pltpu.VMEM((10, 4, 3 * C, Z), BF16),
                pltpu.VMEM((8, 3, C, Z), BF16),
                pltpu.VMEM((6, 4, C, Z), BF16),
                pltpu.VMEM((4, 2, C // 2, Z), BF16),
                pltpu.VMEM((4, 9, 2, C // 2, Z), BF16),
                pltpu.VMEM((4, 8 * C, Z), F32),
                pltpu.VMEM((4, 2, 4 * C, Z), BF16),
                pltpu.VMEM((4, 2, 4 * C, Z), BF16),
                pltpu.VMEM((4, 2, C, Z), F32),
                pltpu.VMEM((8, 4, C, Z), F32),
                pltpu.VMEM((4, 2, C, Z), F32),
                pltpu.VMEM((8, 4, 3 * C, Z), BF16),
                pltpu.VMEM((4, 2, 3 * C, Z), BF16),
                pltpu.VMEM((4, 2, 2 * C, Z), BF16),
                pltpu.VMEM((4, 2, 2 * C, Z), BF16),
                pltpu.VMEM((8, 4, C, Z), F32),
                pltpu.VMEM((4, 2, C, Z), F32),
                pltpu.VMEM((6, 4, C, Z), F32),
                pltpu.VMEM((3 * C, 9 * C), F32),
                pltpu.VMEM((3 * C, 9 * C), F32),
                pltpu.VMEM((plane, rows_a, Z), BF16),
                pltpu.VMEM((plane, rows_b, Z), BF16),
                pltpu.VMEM((plane - 1, rows_a, Z), BF16),
                pltpu.VMEM((plane - 1, rows_b, Z), BF16),
                pltpu.VMEM((cx, rows_a, Z), BF16),
                pltpu.VMEM((cx, rows_b, Z), BF16),
                pltpu.VMEM((plane, rows_a, Z), BF16),
                pltpu.VMEM((plane, rows_b, Z), BF16),
                pltpu.SemaphoreType.DMA((9,)),
                pltpu.SemaphoreType.DMA((4, 8)),
                pltpu.SemaphoreType.DMA((4, 8)),
                pltpu.SemaphoreType.DMA((4, 18)),
                pltpu.SemaphoreType.DMA((4, 18)),
                pltpu.SemaphoreType.DMA((3, 2, 15)),
                pltpu.SemaphoreType.DMA((3, 2, 15)),
            ],
            compiler_params=pltpu.CompilerParams(
                collective_id=0, has_side_effects=True, vmem_limit_bytes=48 * 1024 * 1024
            ),
        )(*inputs)
        return pl.pallas_call(
            finish,
            out_shape=[whole]
            + [jax.ShapeDtypeStruct(s, F32) for s in (three, two, three, two)],
            in_specs=[vmem] * 3,
            out_specs=[hbm] * 5,
            scratch_shapes=[pltpu.VMEM(s, F32) for s in (three, two, three, two)]
            + [pltpu.SemaphoreType.DMA((5,))],
            compiler_params=pltpu.CompilerParams(vmem_limit_bytes=32 * 1024 * 1024),
        )(grad, sums_a, sums_b)

    return jax.shard_map(
        step,
        mesh=mesh,
        in_specs=(P(None, "gx", "gy", "gz"), P(None, "gx", "gy", "gz"), P(), P(), P(), P()),
        out_specs=(P(None, "gx", "gy", "gz"), P(), P(), P(), P()),
        check_vma=False,
    )
```

```python
import functools

import jax
import jax.numpy as jnp
from jax import lax
from jax.experimental import pallas as pl
from jax.experimental.pallas import tpu as pltpu
from jax.sharding import PartitionSpec as P

MESH = pl.DeviceIdType.MESH
F32 = jnp.float32
BF16 = jnp.bfloat16
C = 64
Z = 128
NEG = 0.2

FLAT = [(dx, dy) for dx in (0, 1, -1) for dy in (0, 1, -1)]

SIDES = [(1, 0, 0), (-1, 0, 0)] + [(dx, dy, 0) for dx in (1, -1, 0) for dy in (1, -1)]
ENDS = [(dx, dy, dz) for dx, dy in FLAT[::-1] for dz in (1, -1)]


def act_slope(z):
    e = jnp.exp(-jnp.abs(z))
    q = 1.0 / (1.0 + e)
    sig = jnp.where(z >= 0.0, q, e * q)
    soft = jnp.maximum(z, 0.0) + jnp.log(1.0 + e)
    return NEG * z + (1.0 - NEG) * soft, NEG + (1.0 - NEG) * sig


def dot(a, b):
    return lax.dot_general(a, b, (((1,), (0,)), ((), ())), preferred_element_type=F32)


def dot_nt(a, b):
    return lax.dot_general(a, b, (((1,), (1,)), ((), ())), preferred_element_type=F32)


def roll(v, shift):
    shift = shift % Z
    return v if shift == 0 else pltpu.roll(v, shift, 1)


def lanes(rows):
    return lax.broadcasted_iota(jnp.int32, (rows, Z), 1)


class Level:
    def __init__(self, nx, ny, step, wide):
        self.nx, self.ny, self.step = nx, ny, step
        self.wide = wide

    def at(self, y, x):
        return self.wide * y + x


def put_own(level, v_ref, y, x, pencil):
    v_ref[y + 1, x, C : 2 * C, :] = pencil
    if x + 1 < level.nx:
        v_ref[y + 1, x + 1, 0:C, :] = pencil
    if x >= 1:
        v_ref[y + 1, x - 1, 2 * C : 3 * C, :] = pencil


def spread_y_halo(level, v_ref):
    for y in (0, level.ny + 1):
        for x in range(level.nx):
            if x + 1 < level.nx:
                v_ref[y, x + 1, 0:C, :] = v_ref[y, x, C : 2 * C, :]
            if x >= 1:
                v_ref[y, x - 1, 2 * C : 3 * C, :] = v_ref[y, x, C : 2 * C, :]


def add_face(level, face, y, x, pencil):
    spot = level.at(y + 1, x + 1)
    return jnp.where(lanes(C) // 2 == spot, roll(pencil, 2 * spot + 1), face)


def pack_face(face, z_send):
    odd = lanes(C // 2) % 2 == 1
    top, bottom = face[: C // 2], face[C // 2 :]
    z_send[0] = jnp.where(odd, top, roll(bottom, -1)).astype(BF16)
    z_send[1] = jnp.where(odd, roll(bottom, 1), top).astype(BF16)


def planes(level, z_recv):
    lane = lanes(C // 2)
    spot = lane // 2
    at_y, at_x = spot // level.wide, spot % level.wide

    def side(value, size, d):
        if d == 1:
            return value == 0
        if d == -1:
            return value == size + 1
        return (value >= 1) & (value <= size)

    packed = []
    for which in range(2):
        total = jnp.zeros((C // 2, Z), F32)
        for n, (dx, dy) in enumerate(FLAT):
            shift = -(level.nx * dx) - level.wide * level.ny * dy
            piece = roll(z_recv[n, which].astype(F32), 2 * shift)
            total = jnp.where(side(at_y, level.ny, dy) & side(at_x, level.nx, dx), piece, total)
        packed.append(total)
    low, high = packed
    odd = lane % 2 == 1
    top = jnp.where(odd, roll(low, 1), roll(high, -1))
    bottom = jnp.where(odd, low, high)
    return jnp.concatenate([top, bottom], axis=0)


def pack_ends(near, far, z_send):
    odd = lanes(C) % 2 == 1
    left = lanes(C // 2) < C
    down = jnp.where(odd, far, roll(near, -1))
    up = jnp.where(odd, roll(far, 1), near)
    for n, value in enumerate((down, up)):
        packed = jnp.where(left, value[: C // 2], roll(value[C // 2 :], C))
        z_send[n] = packed.astype(BF16)


def outer_planes(z_recv):
    lane = lanes(C)
    spot = lane // 2
    at_y, at_x = spot // 6, spot % 6
    sides = []
    for which in range(2):
        total = jnp.zeros((C, Z), F32)
        for n, (dx, dy) in enumerate(FLAT):
            first_y, last_y = {0: (2, 5), 1: (0, 1), -1: (6, 7)}[dy]
            first_x = 2 - 2 * dx
            mine = (at_y >= first_y) & (at_y <= last_y) & (at_x >= first_x) & (at_x <= first_x + 1)
            packed = z_recv[n, which].astype(F32)
            value = jnp.concatenate([packed, roll(packed, C)], axis=0)
            total = jnp.where(mine, roll(value, 2 * (14 - 2 * dx - 24 * dy)), total)
        sides.append(total)
    low, high = sides
    odd = lane % 2 == 1
    return jnp.where(odd, roll(low, 1), high), jnp.where(odd, low, roll(high, -1))


def halo_columns(level, plane):
    return jnp.concatenate(
        [roll(plane, -2 * (a + level.wide * b)).astype(BF16) for b in range(3) for a in range(3)],
        axis=0,
    )


def stacked(level, v_ref, y, cols=None):
    return jnp.concatenate(
        [
            jnp.concatenate(
                [v_ref[y + b, x] for x in (range(level.nx) if cols is None else cols)], axis=1
            )
            for b in range(3)
        ],
        axis=0,
    )


def correction(weight, columns):
    p = dot(weight, columns)
    return jnp.where(lanes(C) % 2 == 1, p[:C], p[2 * C :])


def conv_rows(level, weight, v_ref, z_ref, beyond=None, rows=None, cols=None):
    lane = lanes(C)
    cols = range(level.nx) if cols is None else cols
    for y in range(level.ny) if rows is None else rows:
        p = dot(weight, stacked(level, v_ref, y, cols))
        for n, x in enumerate(cols):
            part = p[:, n * Z : (n + 1) * Z]
            left = jnp.where(lane < level.step, 0.0, roll(part[:C], level.step))
            right = jnp.where(lane >= Z - level.step, 0.0, roll(part[2 * C :], -level.step))
            z_ref[y, x] = part[C : 2 * C] + left + right
            if beyond is not None:
                spot = level.at(y, x)
                low = roll(part[2 * C :], 2 * spot + 1)
                high = roll(part[:C], 2 * spot - Z + level.step)
                beyond = jnp.where(lane == 2 * spot + 1, low, beyond)
                beyond = jnp.where(lane == 2 * spot, high, beyond)
    return beyond


def fixed(level, fix, z_ref, y, x):
    lane = lanes(C)
    spot = level.at(y, x)
    share = jnp.where(lane == 0, roll(fix, -(2 * spot + 1)), 0.0)
    share = jnp.where(lane == Z - level.step, roll(fix, -level.step - 2 * spot), share)
    return z_ref[y, x] + share


def taps_along_z(level, grad):
    lane = lanes(C)
    first = jnp.where(lane < Z - level.step, roll(grad, -level.step), 0.0)
    last = jnp.where(lane >= level.step, roll(grad, level.step), 0.0)
    return jnp.concatenate([first, grad, last], axis=0).astype(BF16)


def filter_sum(level, g_ref, face, v_ref, columns):
    lane = lanes(C)
    own = roll(face, -2 * (level.wide + 1))
    none = jnp.zeros((C, Z), F32)
    edge = jnp.concatenate(
        [jnp.where(lane % 2 == 1, own, 0.0), none, jnp.where(lane % 2 == 0, own, 0.0)], axis=0
    ).astype(BF16)
    spots = [(y, x) for y in range(level.ny) for x in range(level.nx)]
    grads = jnp.concatenate([g_ref[y, x] for y, x in spots] + [edge], axis=1)
    sums = []
    for b in range(3):
        ends = columns[b * 3 * C : (b + 1) * 3 * C]
        inputs = jnp.concatenate([v_ref[y + b, x] for y, x in spots] + [ends], axis=1)
        sums.append(dot_nt(grads, inputs))
    return sums


def kernel(
    sizes,
    field_hbm, cot_hbm, wf_hbm, wd_hbm, wc_hbm, wu_hbm,
    out_ref, a_ref, b_ref,
    field_ref, cot_ref, wf_ref, wd_ref, wc_ref, wu_ref,
    w_ff, w_fb, w_cf, w_cb, w_d, w_dt, w_u,
    v_f, v_e, g_c, g_f, both, up_ext,
    zs, zr,
    turn, cot, hid, up_grad, slope_f, slope_d, shifted_f, shifted_c, h_two, g_two, z_f, z_c, z_e,
    s_a, s_b, ra_a, ra_b, rb_a, rb_b, rc_a, rc_b,
    local, side_send, side_recv, end_send, end_recv, sum_send, sum_recv,
):
    cx, cy, cz = sizes
    me = (lax.axis_index("gx"), lax.axis_index("gy"), lax.axis_index("gz"))
    fine, coarse, outer = Level(4, 8, 1, 6), Level(2, 4, 2, 6), Level(4, 6, 2, 6)

    def device(d):
        return tuple(lax.rem(m + (o % n), n) for m, o, n in zip(me, d, sizes))

    first = SIDES + [(0, 0, 1), (0, 0, -1)] + [(i, 0, 0) for i in range(3, cx - 2)]
    partners = sorted({tuple(o % n for o, n in zip(d, sizes)) for d in first})
    barrier = pltpu.get_barrier_semaphore()
    for d in partners:
        pl.semaphore_signal(barrier, inc=1, device_id=device(d), device_id_type=MESH)

    def load_in(src, dst, n):
        copy = pltpu.make_async_copy(src, dst, local.at[n])
        copy.start()
        return copy

    field_in = [load_in(field_hbm.at[:, x], field_ref.at[:, x], x) for x in range(4)]
    cot_in = load_in(cot_hbm, cot_ref, 4)
    w_in = [
        load_in(src, dst, 5 + n)
        for n, (src, dst) in enumerate(
            ((wf_hbm, wf_ref), (wu_hbm, wu_ref), (wd_hbm, wd_ref), (wc_hbm, wc_ref))
        )
    ]

    started = []

    def send(src, dst, send_sem, recv_sem, d):
        copy = pltpu.make_async_remote_copy(
            src_ref=src,
            dst_ref=dst,
            send_sem=send_sem,
            recv_sem=recv_sem,
            device_id=device(d),
            device_id_type=MESH,
        )
        copy.start()
        started.append(copy)
        return copy

    def arrive(copies):
        for copy in copies:
            copy.wait_recv()

    def send_sides(which, views):
        copies = []
        for n, (dx, dy, _) in enumerate(SIDES):
            src, dst = views(dx, dy)
            copies.append(
                send(src, dst, side_send.at[which, n], side_recv.at[which, n], (dx, dy, 0))
            )
        return copies

    def along_axis(size, depth, d):
        src = {0: pl.ds(depth, size), 1: pl.ds(size, depth), -1: pl.ds(depth, depth)}[d]
        dst = {0: pl.ds(depth, size), 1: pl.ds(0, depth), -1: pl.ds(size + depth, depth)}[d]
        return src, dst

    def fine_views(v_ref):
        def views(dx, dy):
            ys, yd = along_axis(8, 1, dy)
            xs = {0: pl.ds(0, 4), 1: pl.ds(3, 1), -1: pl.ds(0, 1)}[dx]
            xd = {0: pl.ds(0, 4), 1: pl.ds(0, 1), -1: pl.ds(3, 1)}[dx]
            rows = pl.ds({0: C, 1: 0, -1: 2 * C}[dx], C)
            return v_ref.at[ys, xs, pl.ds(C, C), :], v_ref.at[yd, xd, rows, :]

        return views

    def up_views(dx, dy):
        (ys, yd), (xs, xd) = along_axis(4, 1, dy), along_axis(2, 1, dx)
        return up_ext.at[ys, xs], up_ext.at[yd, xd]

    def down_views(dx, dy):
        ys, yd = along_axis(4, 2, dy)
        return both.at[ys, 1], both.at[yd, 1 - dx]

    def send_ends(which, some):
        copies = []
        for dx, dy, dz in some:
            n = ENDS.index((dx, dy, dz))
            side = 1 if dz == 1 else 0
            src = zs.at[which, side]
            dst = zr.at[which, FLAT.index((dx, dy)), 1 - side]
            copies.append(send(src, dst, end_send.at[which, n], end_recv.at[which, n], (dx, dy, dz)))
        return copies

    def forward_ends(which):
        copies = []
        for n, (dx, dy) in enumerate(FLAT):
            if n:
                src, dst = zr.at[which, 0], zr.at[which, n]
                copies.append(
                    send(src, dst, end_send.at[which, n], end_recv.at[which, n], (dx, dy, 0))
                )
        return copies

    face = jnp.zeros((C, Z), F32)
    for x in range(4):
        field_in[x].wait()
        turn[x] = field_ref[:, x].astype(F32).reshape(C * 8, Z)
        for y in range(8):
            pencil = turn[x, pl.ds(y, C, stride=8), :]
            put_own(fine, v_f, y, x, pencil.astype(BF16))
            face = add_face(fine, face, y, x, pencil)
    pack_face(face, zs.at[0])

    pl.semaphore_wait(barrier, len(partners))
    ends = send_ends(0, ENDS[-2:])
    sides = send_sides(0, fine_views(v_f))

    eye = (
        lax.broadcasted_iota(jnp.int32, (C, C), 0) == lax.broadcasted_iota(jnp.int32, (C, C), 1)
    ).astype(BF16)

    def flipped(w):
        return dot_nt(eye, w).astype(BF16)

    def layout_3(w_ref, forward, backward):
        for a in range(3):
            for b in range(3):
                for c in range(3):
                    w = w_ref[a, b, c]
                    m = b * 3 + a
                    forward[c * C : (c + 1) * C, m * C : (m + 1) * C] = w
                    m, k = 8 - m, 2 - c
                    backward[k * C : (k + 1) * C, m * C : (m + 1) * C] = flipped(w)

    for copy in w_in:
        copy.wait()
    layout_3(wf_ref, w_ff, w_fb)
    arrive(ends)
    forwards = forward_ends(0)
    layout_3(wc_ref, w_cf, w_cb)
    for a in range(2):
        for b in range(2):
            for c in range(2):
                m = b * 2 + a
                w = wd_ref[a, b, c]
                w_d[c * C : (c + 1) * C, m * C : (m + 1) * C] = w
                w_dt[m * C : (m + 1) * C, c * C : (c + 1) * C] = flipped(w)
                w_u[c * C : (c + 1) * C, m * C : (m + 1) * C] = flipped(wu_ref[a, b, c])

    def pair(ref, y):
        return jnp.concatenate([ref[y, 0], ref[y, 1]], axis=1)

    cot_in.wait()
    for x in range(4):
        turn[x] = cot_ref[:, x].astype(F32).reshape(C * 8, Z)
        for y in range(8):
            m = (y % 2) * 2 + x % 2
            pencil = turn[x, pl.ds(y, C, stride=8), :]
            cot[y // 2, x // 2, m * C : (m + 1) * C, :] = pencil.astype(BF16)
    even = lanes(C) % 2 == 0
    odd = lanes(C) % 2 == 1
    face = jnp.zeros((C, Z), F32)
    for y in range(4):
        p = dot(w_u[...], pair(cot, y))
        for x in range(2):
            part = p[:, x * Z : (x + 1) * Z]
            g = part[:C] + roll(part[C:], -1)
            up_grad[y, x] = g
            up_ext[y + 1, x + 1] = g.astype(BF16)
            face = add_face(coarse, face, y, x, jnp.where(even, g, roll(g, 1)))
    pack_face(face, zs.at[1])

    conv_rows(fine, w_ff[...], v_f, z_f, rows=range(1, 7), cols=(1, 2))
    arrive(sides)
    spread_y_halo(fine, v_f)
    conv_rows(fine, w_ff[...], v_f, z_f, rows=(0, 7))
    conv_rows(fine, w_ff[...], v_f, z_f, rows=range(1, 7), cols=(0, 3))
    up_ends = send_ends(1, ENDS[-2:])
    up_sides = send_sides(1, up_views)
    arrive(forwards)
    columns_f = halo_columns(fine, planes(fine, zr.at[0]))
    fix = correction(w_ff[...], columns_f)
    for y in range(8):
        for x in range(4):
            h, s = act_slope(fixed(fine, fix, z_f, y, x))
            m = (y % 2) * 2 + x % 2
            hid[y // 2, x // 2, m * C : (m + 1) * C, :] = h.astype(BF16)
            slope_f[y, x] = s

    lane = lanes(C)
    near = jnp.zeros((C, Z), F32)
    far = jnp.zeros((C, Z), F32)
    for y in range(4):
        p = dot(w_d[...], pair(hid, y))
        row = []
        for x in range(2):
            part = p[:, x * Z : (x + 1) * Z]
            d, s = act_slope(part[:C] + roll(part[C:], -1))
            slope_d[y, x] = s
            row.append(d)
            spot = coarse.at(y, x)
            near = jnp.where(
                lane // 2 == spot, roll(jnp.where(even, d, roll(d, 1)), 2 * spot + 1), near
            )
            far = jnp.where(lane == 2 * spot + 1, roll(d, 2 * spot - 1), far)
            far = jnp.where(lane == 2 * spot, roll(d, 2 * spot - 124), far)
        both[y + 2, 1] = jnp.where(even, row[0], roll(row[1], 1)).astype(BF16)
    pack_ends(near, far, zs.at[2])
    sides = send_sides(2, down_views)
    ends = send_ends(2, ENDS)

    arrive(up_ends)
    forwards = forward_ends(1)

    def unpack(y, block):
        value = both[y, block]
        moved = roll(value.astype(F32), -1).astype(BF16)
        for x, pencil in ((2 * block, value), (2 * block + 1, moved)):
            for a in range(3):
                if 0 <= x - a < 4:
                    v_e[y, x - a, a * C : (a + 1) * C, :] = pencil

    for y in range(4):
        unpack(y + 2, 1)
    arrive(sides)
    for y in range(8):
        for block in range(3):
            if block != 1 or not 2 <= y < 6:
                unpack(y, block)
    beyond = conv_rows(outer, w_cf[...], v_e, z_e, jnp.zeros((C, Z), F32))
    arrive(ends)
    plane_1, plane_2 = outer_planes(zr.at[2])
    p_1 = dot(w_cf[...], halo_columns(outer, plane_1))
    p_2 = dot(w_cf[...], halo_columns(outer, plane_2))
    columns_c = halo_columns(outer, roll(plane_1, -14))
    fix = jnp.where(odd, p_1[:C], p_1[2 * C :])
    beyond = beyond + p_1[C : 2 * C] + jnp.where(odd, p_2[:C], p_2[2 * C :])
    arrive(up_sides)
    face = jnp.zeros((C, Z), F32)
    for y in range(6):
        for x in range(4):
            h, s = act_slope(fixed(outer, fix, z_e, y, x))
            own = 1 <= y < 5 and 1 <= x < 3
            up = up_grad[y - 1, x - 1] if own else up_ext[y, x].astype(F32)
            g = jnp.where(even, up * s, 0.0).astype(BF16).astype(F32)
            for a in range(3):
                if 0 <= x - a < 2:
                    g_c[y, x - a, a * C : (a + 1) * C, :] = g.astype(BF16)
            if own:
                h = jnp.where(even, h, 0.0)
                h_two[y - 1, x - 1] = jnp.concatenate([h, roll(h, 1)], axis=0).astype(BF16)
                shifted_c[y - 1, x - 1] = taps_along_z(coarse, g)
                face = add_face(coarse, face, y - 1, x - 1, jnp.where(even, g, roll(g, 1)))
    arrive(forwards)
    g_plane = planes(coarse, zr.at[1]) * act_slope(beyond)[1]
    g_plane = g_plane.astype(BF16).astype(F32)

    def long(ref):
        return jnp.concatenate([ref[y, x] for y in range(4) for x in range(2)], axis=1)

    def place(ref, row):
        chunk = ref.shape[1]
        return row // chunk, pl.ds(row % chunk, 16), slice(None)

    def store(ref, block, value):
        for at in range(0, C, 16):
            ref[place(ref, block * C + at)] = value[at : at + 16].astype(BF16)

    def pack_sums(sums, ref):
        parts = [sums[b][c * C : (c + 1) * C] for c in range(3) for b in range(3)]
        tails = [part[:, Z:] for part in parts] + [jnp.zeros((C, C), F32)]
        for j, part in enumerate(parts):
            store(ref, j, part[:, :Z])
        for q in range(5):
            store(ref, 9 + q, jnp.concatenate(tails[2 * q : 2 * q + 2], axis=1))
        for block in (18, 19):
            store(ref, block, jnp.zeros((C, Z), F32))

    in_plane = [(0, j, k) for j in range(cy) for k in range(cz) if (j, k) != (0, 0)]
    in_plane.sort(key=lambda d: -min(d[1], cy - d[1]) - min(d[2], cz - d[2]))
    in_line = sorted([(i, 0, 0) for i in range(1, cx)], key=lambda d: -min(d[0], cx - d[0]))
    plane_at = me[1] * cz + me[2]
    voxels = 4 * 8 * Z * cx * cy * cz
    scale = 1.0 / (voxels**0.5)

    def send_sum(src, dst, stage, which, n, d):
        return send(src, dst, sum_send.at[stage, which, n], sum_recv.at[stage, which, n], d)

    def scatter(which, s, ra):
        out = []
        for n, d in enumerate(in_plane):
            there = device(d)
            out.append(send_sum(s.at[there[1] * cz + there[2]], ra.at[n], 0, which, n, d))
        return out

    def along(which, s, ra, rb, waits):
        arrive(waits)
        total = s[plane_at].astype(F32)
        for n in range(len(in_plane)):
            total = total + ra[n].astype(F32)
        rb[me[0]] = total.astype(BF16)
        return [
            send_sum(rb.at[me[0]], rb.at[me[0]], 1, which, n, d) for n, d in enumerate(in_line)
        ]

    def gather(which, rb, rc, waits):
        arrive(waits)
        total = rb[0].astype(F32)
        for n in range(1, cx):
            total = total + rb[n].astype(F32)
        rc[plane_at] = (total * scale).astype(BF16)
        return [
            send_sum(rc.at[plane_at], rc.at[plane_at], 2, which, n, d)
            for n, d in enumerate(in_plane)
        ]

    inner = v_e.at[pl.ds(1, 6), pl.ds(1, 2)]
    pack_sums(filter_sum(coarse, shifted_c, face, inner, columns_c), s_a)
    p = dot_nt(long(cot), long(h_two))
    for m in range(4):
        store(s_a, 14 + m, p[m * C : (m + 1) * C])
    waits_a = scatter(0, s_a, ra_a)

    conv_rows(coarse, w_cb[...], g_c, z_c)
    fix = correction(w_cb[...], halo_columns(coarse, g_plane))
    for y in range(4):
        for x in range(2):
            g = jnp.where(even, fixed(coarse, fix, z_c, y, x) * slope_d[y, x], 0.0)
            g_two[y, x] = jnp.concatenate([g, roll(g, 1)], axis=0).astype(BF16)

    face = jnp.zeros((C, Z), F32)
    for half in range(4):
        p = dot(w_dt[...], pair(g_two, half))
        for b in range(2):
            y = half * 2 + b
            for x in range(4):
                m = b * 2 + x % 2
                wide = p[m * C : (m + 1) * C, (x // 2) * Z : (x // 2 + 1) * Z]
                c = cot[half, x // 2, m * C : (m + 1) * C, :].astype(F32)
                g = ((c + wide) * slope_f[y, x]).astype(BF16).astype(F32)
                put_own(fine, g_f, y, x, g.astype(BF16))
                shifted_f[y, x] = taps_along_z(fine, g)
                face = add_face(fine, face, y, x, g)
    pack_face(face, zs.at[3])

    pack_sums(filter_sum(fine, shifted_f, face, v_f, columns_f), s_b)
    p = dot_nt(long(g_two), long(hid))
    for c in range(2):
        for b in range(2):
            store(s_b, 14 + c * 2 + b, p[c * C : (c + 1) * C, b * Z : (b + 1) * Z])
    waits_b = scatter(1, s_b, ra_b)
    ends = send_ends(3, ENDS[-2:])
    sides = send_sides(3, fine_views(g_f))

    waits_a = along(0, s_a, ra_a, rb_a, waits_a)
    arrive(ends)
    forwards = forward_ends(3)
    waits_b = along(1, s_b, ra_b, rb_b, waits_b)
    waits_a = gather(0, rb_a, rc_a, waits_a)
    arrive(sides)
    spread_y_halo(fine, g_f)
    conv_rows(fine, w_fb[...], g_f, z_f)
    waits_b = gather(1, rb_b, rc_b, waits_b)
    arrive(forwards)
    fix = correction(w_fb[...], halo_columns(fine, planes(fine, zr.at[3])))
    for x in range(4):
        for y in range(8):
            turn[x, pl.ds(y, C, stride=8), :] = fixed(fine, fix, z_f, y, x)
        out_ref[:, x] = turn[x].reshape(C, 8, Z).astype(BF16)
    arrive(waits_a)
    a_ref[...] = rc_a[...]
    arrive(waits_b)
    b_ref[...] = rc_b[...]
    for copy in started:
        copy.wait_send()


def finish(
    field_ref, a_ref, b_ref,
    out_hbm, of_hbm, od_hbm, oc_hbm, ou_hbm,
    of_ref, od_ref, oc_ref, ou_ref,
    sems,
):
    copies = []

    def write(src, dst):
        copy = pltpu.make_async_copy(src, dst, sems.at[len(copies)])
        copy.start()
        copies.append(copy)

    write(field_ref, out_hbm)

    def load(ref, block):
        rows = []
        for at in range(block * C, (block + 1) * C, 16):
            rows.append(ref[at // ref.shape[1], pl.ds(at % ref.shape[1], 16), :])
        return jnp.concatenate(rows, axis=0).astype(F32)

    def unpack_sums(ref, o_ref):
        for block in range(14):
            value = load(ref, block)
            for half in range(2):
                j, a = (block, half) if block < 9 else (2 * (block - 9) + half, 2)
                if j < 9:
                    o_ref[a, j % 3, j // 3] = value[:, half * C : (half + 1) * C]

    unpack_sums(a_ref, oc_ref)
    write(oc_ref, oc_hbm)
    unpack_sums(b_ref, of_ref)
    write(of_ref, of_hbm)
    for m in range(4):
        value = load(a_ref, 14 + m)
        for c in range(2):
            ou_ref[m % 2, m // 2, c] = value[:, c * C : (c + 1) * C]
    write(ou_ref, ou_hbm)
    for c in range(2):
        for b in range(2):
            value = load(b_ref, 14 + c * 2 + b)
            for a in range(2):
                od_ref[a, b, c] = value[:, a * C : (a + 1) * C]
    write(od_ref, od_hbm)
    for copy in copies:
        copy.wait()


def solution(mesh):
    sizes = (mesh.shape["gx"], mesh.shape["gy"], mesh.shape["gz"])
    cx, cy, cz = sizes
    plane = cy * cz
    rows_a, rows_b = 20 * C // plane, 20 * C // plane

    def step(field, cotangent, w_fine, w_down, w_coarse, w_up):
        vmem = pl.BlockSpec(memory_space=pltpu.VMEM)
        hbm = pl.BlockSpec(memory_space=pltpu.HBM)
        three, two = (3, 3, 3, C, C), (2, 2, 2, C, C)
        packed = [jax.ShapeDtypeStruct((plane, rows, Z), BF16) for rows in (rows_a, rows_b)]
        whole = jax.ShapeDtypeStruct((C, 4, 8, Z), BF16)
        inputs = [
            pltpu.with_memory_space_constraint(v, pltpu.HBM)
            for v in (field, cotangent, w_fine, w_down, w_coarse, w_up)
        ]
        grad, sums_a, sums_b = pl.pallas_call(
            functools.partial(kernel, sizes),
            out_shape=[whole, *packed],
            in_specs=[hbm] * 6,
            out_specs=[vmem] * 3,
            scratch_shapes=[
                pltpu.VMEM((C, 4, 8, Z), BF16),
                pltpu.VMEM((C, 4, 8, Z), BF16),
                pltpu.VMEM(three, BF16),
                pltpu.VMEM(two, BF16),
                pltpu.VMEM(three, BF16),
                pltpu.VMEM(two, BF16),
                pltpu.VMEM((3 * C, 9 * C), BF16),
                pltpu.VMEM((3 * C, 9 * C), BF16),
                pltpu.VMEM((3 * C, 9 * C), BF16),
                pltpu.VMEM((3 * C, 9 * C), BF16),
                pltpu.VMEM((2 * C, 4 * C), BF16),
                pltpu.VMEM((4 * C, 2 * C), BF16),
                pltpu.VMEM((2 * C, 4 * C), BF16),
                pltpu.VMEM((10, 4, 3 * C, Z), BF16),
                pltpu.VMEM((8, 4, 3 * C, Z), BF16),
                pltpu.VMEM((6, 2, 3 * C, Z), BF16),
                pltpu.VMEM((10, 4, 3 * C, Z), BF16),
                pltpu.VMEM((8, 3, C, Z), BF16),
                pltpu.VMEM((6, 4, C, Z), BF16),
                pltpu.VMEM((4, 2, C // 2, Z), BF16),
                pltpu.VMEM((4, 9, 2, C // 2, Z), BF16),
                pltpu.VMEM((4, 8 * C, Z), F32),
                pltpu.VMEM((4, 2, 4 * C, Z), BF16),
                pltpu.VMEM((4, 2, 4 * C, Z), BF16),
                pltpu.VMEM((4, 2, C, Z), F32),
                pltpu.VMEM((8, 4, C, Z), F32),
                pltpu.VMEM((4, 2, C, Z), F32),
                pltpu.VMEM((8, 4, 3 * C, Z), BF16),
                pltpu.VMEM((4, 2, 3 * C, Z), BF16),
                pltpu.VMEM((4, 2, 2 * C, Z), BF16),
                pltpu.VMEM((4, 2, 2 * C, Z), BF16),
                pltpu.VMEM((8, 4, C, Z), F32),
                pltpu.VMEM((4, 2, C, Z), F32),
                pltpu.VMEM((6, 4, C, Z), F32),
                pltpu.VMEM((plane, rows_a, Z), BF16),
                pltpu.VMEM((plane, rows_b, Z), BF16),
                pltpu.VMEM((plane - 1, rows_a, Z), BF16),
                pltpu.VMEM((plane - 1, rows_b, Z), BF16),
                pltpu.VMEM((cx, rows_a, Z), BF16),
                pltpu.VMEM((cx, rows_b, Z), BF16),
                pltpu.VMEM((plane, rows_a, Z), BF16),
                pltpu.VMEM((plane, rows_b, Z), BF16),
                pltpu.SemaphoreType.DMA((9,)),
                pltpu.SemaphoreType.DMA((4, 8)),
                pltpu.SemaphoreType.DMA((4, 8)),
                pltpu.SemaphoreType.DMA((4, 18)),
                pltpu.SemaphoreType.DMA((4, 18)),
                pltpu.SemaphoreType.DMA((3, 2, 15)),
                pltpu.SemaphoreType.DMA((3, 2, 15)),
            ],
            compiler_params=pltpu.CompilerParams(
                collective_id=0, has_side_effects=True, vmem_limit_bytes=48 * 1024 * 1024
            ),
        )(*inputs)
        return pl.pallas_call(
            finish,
            out_shape=[whole]
            + [jax.ShapeDtypeStruct(s, F32) for s in (three, two, three, two)],
            in_specs=[vmem] * 3,
            out_specs=[hbm] * 5,
            scratch_shapes=[pltpu.VMEM(s, F32) for s in (three, two, three, two)]
            + [pltpu.SemaphoreType.DMA((5,))],
            compiler_params=pltpu.CompilerParams(vmem_limit_bytes=32 * 1024 * 1024),
        )(grad, sums_a, sums_b)

    return jax.shard_map(
        step,
        mesh=mesh,
        in_specs=(P(None, "gx", "gy", "gz"), P(None, "gx", "gy", "gz"), P(), P(), P(), P()),
        out_specs=(P(None, "gx", "gy", "gz"), P(), P(), P(), P()),
        check_vma=False,
    )
```

```python
import functools

import jax
import jax.numpy as jnp
from jax import lax
from jax.experimental import pallas as pl
from jax.experimental.pallas import tpu as pltpu
from jax.sharding import PartitionSpec as P

MESH = pl.DeviceIdType.MESH
F32 = jnp.float32
BF16 = jnp.bfloat16
C = 64
Z = 128
NEG = 0.2

FLAT = [(dx, dy) for dx in (0, 1, -1) for dy in (0, 1, -1)]

SIDES = [(1, 0, 0), (-1, 0, 0)] + [(dx, dy, 0) for dx in (1, -1, 0) for dy in (1, -1)]
ENDS = [(dx, dy, dz) for dx, dy in FLAT[::-1] for dz in (1, -1)]


def act_slope(z):
    e = jnp.exp(-jnp.abs(z))
    q = 1.0 / (1.0 + e)
    sig = jnp.where(z >= 0.0, q, e * q)
    soft = jnp.maximum(z, 0.0) + jnp.log(1.0 + e)
    return NEG * z + (1.0 - NEG) * soft, NEG + (1.0 - NEG) * sig


def dot(a, b):
    return lax.dot_general(a, b, (((1,), (0,)), ((), ())), preferred_element_type=F32)


def dot_nt(a, b):
    return lax.dot_general(a, b, (((1,), (1,)), ((), ())), preferred_element_type=F32)


def roll(v, shift):
    shift = shift % Z
    return v if shift == 0 else pltpu.roll(v, shift, 1)


def lanes(rows):
    return lax.broadcasted_iota(jnp.int32, (rows, Z), 1)


class Level:
    def __init__(self, nx, ny, step, wide):
        self.nx, self.ny, self.step = nx, ny, step
        self.wide = wide

    def at(self, y, x):
        return self.wide * y + x


def put_own(level, v_ref, y, x, pencil):
    v_ref[y + 1, x, C : 2 * C, :] = pencil
    if x + 1 < level.nx:
        v_ref[y + 1, x + 1, 0:C, :] = pencil
    if x >= 1:
        v_ref[y + 1, x - 1, 2 * C : 3 * C, :] = pencil


def spread_y_halo(level, v_ref):
    for y in (0, level.ny + 1):
        for x in range(level.nx):
            if x + 1 < level.nx:
                v_ref[y, x + 1, 0:C, :] = v_ref[y, x, C : 2 * C, :]
            if x >= 1:
                v_ref[y, x - 1, 2 * C : 3 * C, :] = v_ref[y, x, C : 2 * C, :]


def add_face(level, face, y, x, pencil):
    spot = level.at(y + 1, x + 1)
    return jnp.where(lanes(C) // 2 == spot, roll(pencil, 2 * spot + 1), face)


def pack_face(face, z_send):
    odd = lanes(C // 2) % 2 == 1
    top, bottom = face[: C // 2], face[C // 2 :]
    z_send[0] = jnp.where(odd, top, roll(bottom, -1)).astype(BF16)
    z_send[1] = jnp.where(odd, roll(bottom, 1), top).astype(BF16)


def planes(level, z_recv):
    lane = lanes(C // 2)
    spot = lane // 2
    at_y, at_x = spot // level.wide, spot % level.wide

    def side(value, size, d):
        if d == 1:
            return value == 0
        if d == -1:
            return value == size + 1
        return (value >= 1) & (value <= size)

    packed = []
    for which in range(2):
        total = jnp.zeros((C // 2, Z), F32)
        for n, (dx, dy) in enumerate(FLAT):
            shift = -(level.nx * dx) - level.wide * level.ny * dy
            piece = roll(z_recv[n, which].astype(F32), 2 * shift)
            total = jnp.where(side(at_y, level.ny, dy) & side(at_x, level.nx, dx), piece, total)
        packed.append(total)
    low, high = packed
    odd = lane % 2 == 1
    top = jnp.where(odd, roll(low, 1), roll(high, -1))
    bottom = jnp.where(odd, low, high)
    return jnp.concatenate([top, bottom], axis=0)


def pack_ends(near, far, z_send):
    odd = lanes(C) % 2 == 1
    left = lanes(C // 2) < C
    down = jnp.where(odd, far, roll(near, -1))
    up = jnp.where(odd, roll(far, 1), near)
    for n, value in enumerate((down, up)):
        packed = jnp.where(left, value[: C // 2], roll(value[C // 2 :], C))
        z_send[n] = packed.astype(BF16)


def outer_planes(z_recv):
    lane = lanes(C)
    spot = lane // 2
    at_y, at_x = spot // 6, spot % 6
    sides = []
    for which in range(2):
        total = jnp.zeros((C, Z), F32)
        for n, (dx, dy) in enumerate(FLAT):
            first_y, last_y = {0: (2, 5), 1: (0, 1), -1: (6, 7)}[dy]
            first_x = 2 - 2 * dx
            mine = (at_y >= first_y) & (at_y <= last_y) & (at_x >= first_x) & (at_x <= first_x + 1)
            packed = z_recv[n, which].astype(F32)
            value = jnp.concatenate([packed, roll(packed, C)], axis=0)
            total = jnp.where(mine, roll(value, 2 * (14 - 2 * dx - 24 * dy)), total)
        sides.append(total)
    low, high = sides
    odd = lane % 2 == 1
    return jnp.where(odd, roll(low, 1), high), jnp.where(odd, low, roll(high, -1))


def halo_columns(level, plane):
    return jnp.concatenate(
        [roll(plane, -2 * (a + level.wide * b)).astype(BF16) for b in range(3) for a in range(3)],
        axis=0,
    )


def stacked(level, v_ref, y, cols=None):
    return jnp.concatenate(
        [
            jnp.concatenate(
                [v_ref[y + b, x] for x in (range(level.nx) if cols is None else cols)], axis=1
            )
            for b in range(3)
        ],
        axis=0,
    )


def correction(weight, columns):
    p = dot(weight, columns)
    return jnp.where(lanes(C) % 2 == 1, p[:C], p[2 * C :])


def conv_rows(level, weight, v_ref, z_ref, beyond=None, rows=None, cols=None):
    lane = lanes(C)
    cols = range(level.nx) if cols is None else cols
    for y in range(level.ny) if rows is None else rows:
        p = dot(weight, stacked(level, v_ref, y, cols))
        for n, x in enumerate(cols):
            part = p[:, n * Z : (n + 1) * Z]
            left = jnp.where(lane < level.step, 0.0, roll(part[:C], level.step))
            right = jnp.where(lane >= Z - level.step, 0.0, roll(part[2 * C :], -level.step))
            z_ref[y, x] = part[C : 2 * C] + left + right
            if beyond is not None:
                spot = level.at(y, x)
                low = roll(part[2 * C :], 2 * spot + 1)
                high = roll(part[:C], 2 * spot - Z + level.step)
                beyond = jnp.where(lane == 2 * spot + 1, low, beyond)
                beyond = jnp.where(lane == 2 * spot, high, beyond)
    return beyond


def fixed(level, fix, z_ref, y, x):
    lane = lanes(C)
    spot = level.at(y, x)
    share = jnp.where(lane == 0, roll(fix, -(2 * spot + 1)), 0.0)
    share = jnp.where(lane == Z - level.step, roll(fix, -level.step - 2 * spot), share)
    return z_ref[y, x] + share


def taps_along_z(level, grad):
    lane = lanes(C)
    first = jnp.where(lane < Z - level.step, roll(grad, -level.step), 0.0)
    last = jnp.where(lane >= level.step, roll(grad, level.step), 0.0)
    return jnp.concatenate([first, grad, last], axis=0).astype(BF16)


def filter_sum(level, g_ref, face, v_ref, columns):
    lane = lanes(C)
    own = roll(face, -2 * (level.wide + 1))
    none = jnp.zeros((C, Z), F32)
    edge = jnp.concatenate(
        [jnp.where(lane % 2 == 1, own, 0.0), none, jnp.where(lane % 2 == 0, own, 0.0)], axis=0
    ).astype(BF16)
    spots = [(y, x) for y in range(level.ny) for x in range(level.nx)]
    grads = jnp.concatenate([g_ref[y, x] for y, x in spots] + [edge], axis=1)
    sums = []
    for b in range(3):
        ends = columns[b * 3 * C : (b + 1) * 3 * C]
        inputs = jnp.concatenate([v_ref[y + b, x] for y, x in spots] + [ends], axis=1)
        sums.append(dot_nt(grads, inputs))
    return sums


def kernel(
    sizes,
    field_hbm, cot_hbm, wf_hbm, wd_hbm, wc_hbm, wu_hbm,
    out_ref, a_ref, b_ref,
    field_ref, cot_ref, wf_ref, wd_ref, wc_ref, wu_ref,
    w_ff, w_fb, w_cf, w_cb, w_d, w_dt, w_u,
    v_f, v_e, g_c, g_f, both, up_ext,
    zs, zr,
    turn, cot, hid, up_grad, slope_f, slope_d, shifted_f, shifted_c, h_two, g_two, z_f, z_c, z_e,
    s_a, s_b, ra_a, ra_b, rb_a, rb_b, rc_a, rc_b,
    local, side_send, side_recv, end_send, end_recv, sum_send, sum_recv,
):
    cx, cy, cz = sizes
    me = (lax.axis_index("gx"), lax.axis_index("gy"), lax.axis_index("gz"))
    fine, coarse, outer = Level(4, 8, 1, 6), Level(2, 4, 2, 6), Level(4, 6, 2, 6)

    def device(d):
        return tuple(lax.rem(m + (o % n), n) for m, o, n in zip(me, d, sizes))

    first = SIDES + [(0, 0, 1), (0, 0, -1)] + [(i, 0, 0) for i in range(3, cx - 2)]
    partners = sorted({tuple(o % n for o, n in zip(d, sizes)) for d in first})
    barrier = pltpu.get_barrier_semaphore()
    for d in partners:
        pl.semaphore_signal(barrier, inc=1, device_id=device(d), device_id_type=MESH)

    def load_in(src, dst, n):
        copy = pltpu.make_async_copy(src, dst, local.at[n])
        copy.start()
        return copy

    field_in = [load_in(field_hbm.at[:, x], field_ref.at[:, x], x) for x in range(4)]
    cot_in = load_in(cot_hbm, cot_ref, 4)
    w_in = [
        load_in(src, dst, 5 + n)
        for n, (src, dst) in enumerate(
            ((wf_hbm, wf_ref), (wu_hbm, wu_ref), (wd_hbm, wd_ref), (wc_hbm, wc_ref))
        )
    ]

    started = []

    def send(src, dst, send_sem, recv_sem, d):
        copy = pltpu.make_async_remote_copy(
            src_ref=src,
            dst_ref=dst,
            send_sem=send_sem,
            recv_sem=recv_sem,
            device_id=device(d),
            device_id_type=MESH,
        )
        copy.start()
        started.append(copy)
        return copy

    def arrive(copies):
        for copy in copies:
            copy.wait_recv()

    def send_sides(which, views):
        copies = []
        for n, (dx, dy, _) in enumerate(SIDES):
            src, dst = views(dx, dy)
            copies.append(
                send(src, dst, side_send.at[which, n], side_recv.at[which, n], (dx, dy, 0))
            )
        return copies

    def along_axis(size, depth, d):
        src = {0: pl.ds(depth, size), 1: pl.ds(size, depth), -1: pl.ds(depth, depth)}[d]
        dst = {0: pl.ds(depth, size), 1: pl.ds(0, depth), -1: pl.ds(size + depth, depth)}[d]
        return src, dst

    def fine_views(v_ref):
        def views(dx, dy):
            ys, yd = along_axis(8, 1, dy)
            xs = {0: pl.ds(0, 4), 1: pl.ds(3, 1), -1: pl.ds(0, 1)}[dx]
            xd = {0: pl.ds(0, 4), 1: pl.ds(0, 1), -1: pl.ds(3, 1)}[dx]
            rows = pl.ds({0: C, 1: 0, -1: 2 * C}[dx], C)
            return v_ref.at[ys, xs, pl.ds(C, C), :], v_ref.at[yd, xd, rows, :]

        return views

    def up_views(dx, dy):
        (ys, yd), (xs, xd) = along_axis(4, 1, dy), along_axis(2, 1, dx)
        return up_ext.at[ys, xs], up_ext.at[yd, xd]

    def down_views(dx, dy):
        ys, yd = along_axis(4, 2, dy)
        return both.at[ys, 1], both.at[yd, 1 - dx]

    def send_ends(which, some):
        copies = []
        for dx, dy, dz in some:
            n = ENDS.index((dx, dy, dz))
            side = 1 if dz == 1 else 0
            src = zs.at[which, side]
            dst = zr.at[which, FLAT.index((dx, dy)), 1 - side]
            copies.append(send(src, dst, end_send.at[which, n], end_recv.at[which, n], (dx, dy, dz)))
        return copies

    def forward_ends(which):
        copies = []
        for n, (dx, dy) in enumerate(FLAT):
            if n:
                src, dst = zr.at[which, 0], zr.at[which, n]
                copies.append(
                    send(src, dst, end_send.at[which, n], end_recv.at[which, n], (dx, dy, 0))
                )
        return copies

    face = jnp.zeros((C, Z), F32)
    for x in range(4):
        field_in[x].wait()
        turn[x] = field_ref[:, x].astype(F32).reshape(C * 8, Z)
        for y in range(8):
            pencil = turn[x, pl.ds(y, C, stride=8), :]
            put_own(fine, v_f, y, x, pencil.astype(BF16))
            face = add_face(fine, face, y, x, pencil)
    pack_face(face, zs.at[0])

    pl.semaphore_wait(barrier, len(partners))
    ends = send_ends(0, ENDS[-2:])
    sides = send_sides(0, fine_views(v_f))

    eye = (
        lax.broadcasted_iota(jnp.int32, (C, C), 0) == lax.broadcasted_iota(jnp.int32, (C, C), 1)
    ).astype(BF16)

    def flipped(w):
        return dot_nt(eye, w).astype(BF16)

    def layout_3(w_ref, forward, backward):
        for a in range(3):
            for b in range(3):
                for c in range(3):
                    w = w_ref[a, b, c]
                    m = b * 3 + a
                    forward[c * C : (c + 1) * C, m * C : (m + 1) * C] = w
                    m, k = 8 - m, 2 - c
                    backward[k * C : (k + 1) * C, m * C : (m + 1) * C] = flipped(w)

    for copy in w_in:
        copy.wait()
    layout_3(wf_ref, w_ff, w_fb)
    arrive(ends)
    forwards = forward_ends(0)
    layout_3(wc_ref, w_cf, w_cb)
    for a in range(2):
        for b in range(2):
            for c in range(2):
                m = b * 2 + a
                w = wd_ref[a, b, c]
                w_d[c * C : (c + 1) * C, m * C : (m + 1) * C] = w
                w_dt[m * C : (m + 1) * C, c * C : (c + 1) * C] = flipped(w)
                w_u[c * C : (c + 1) * C, m * C : (m + 1) * C] = flipped(wu_ref[a, b, c])

    def pair(ref, y):
        return jnp.concatenate([ref[y, 0], ref[y, 1]], axis=1)

    cot_in.wait()
    for x in range(4):
        turn[x] = cot_ref[:, x].astype(F32).reshape(C * 8, Z)
        for y in range(8):
            m = (y % 2) * 2 + x % 2
            pencil = turn[x, pl.ds(y, C, stride=8), :]
            cot[y // 2, x // 2, m * C : (m + 1) * C, :] = pencil.astype(BF16)
    even = lanes(C) % 2 == 0
    odd = lanes(C) % 2 == 1
    face = jnp.zeros((C, Z), F32)
    for y in range(4):
        p = dot(w_u[...], pair(cot, y))
        for x in range(2):
            part = p[:, x * Z : (x + 1) * Z]
            g = part[:C] + roll(part[C:], -1)
            up_grad[y, x] = g
            up_ext[y + 1, x + 1] = g.astype(BF16)
            face = add_face(coarse, face, y, x, jnp.where(even, g, roll(g, 1)))
    pack_face(face, zs.at[1])

    conv_rows(fine, w_ff[...], v_f, z_f, rows=range(1, 7), cols=(1, 2))
    arrive(sides)
    spread_y_halo(fine, v_f)
    conv_rows(fine, w_ff[...], v_f, z_f, rows=(0, 7))
    conv_rows(fine, w_ff[...], v_f, z_f, rows=range(1, 7), cols=(0, 3))
    up_ends = send_ends(1, ENDS[-2:])
    up_sides = send_sides(1, up_views)
    arrive(forwards)
    columns_f = halo_columns(fine, planes(fine, zr.at[0]))
    fix = correction(w_ff[...], columns_f)
    for y in range(8):
        for x in range(4):
            h, s = act_slope(fixed(fine, fix, z_f, y, x))
            m = (y % 2) * 2 + x % 2
            hid[y // 2, x // 2, m * C : (m + 1) * C, :] = h.astype(BF16)
            slope_f[y, x] = s

    lane = lanes(C)
    near = jnp.zeros((C, Z), F32)
    far = jnp.zeros((C, Z), F32)
    for y in range(4):
        p = dot(w_d[...], pair(hid, y))
        row = []
        for x in range(2):
            part = p[:, x * Z : (x + 1) * Z]
            d, s = act_slope(part[:C] + roll(part[C:], -1))
            slope_d[y, x] = s
            row.append(d)
            spot = coarse.at(y, x)
            near = jnp.where(
                lane // 2 == spot, roll(jnp.where(even, d, roll(d, 1)), 2 * spot + 1), near
            )
            far = jnp.where(lane == 2 * spot + 1, roll(d, 2 * spot - 1), far)
            far = jnp.where(lane == 2 * spot, roll(d, 2 * spot - 124), far)
        both[y + 2, 1] = jnp.where(even, row[0], roll(row[1], 1)).astype(BF16)
    pack_ends(near, far, zs.at[2])
    sides = send_sides(2, down_views)
    ends = send_ends(2, ENDS)

    arrive(up_ends)
    forwards = forward_ends(1)

    def unpack(y, block):
        value = both[y, block]
        moved = roll(value.astype(F32), -1).astype(BF16)
        for x, pencil in ((2 * block, value), (2 * block + 1, moved)):
            for a in range(3):
                if 0 <= x - a < 4:
                    v_e[y, x - a, a * C : (a + 1) * C, :] = pencil

    for y in range(4):
        unpack(y + 2, 1)
    arrive(sides)
    for y in range(8):
        for block in range(3):
            if block != 1 or not 2 <= y < 6:
                unpack(y, block)
    beyond = conv_rows(outer, w_cf[...], v_e, z_e, jnp.zeros((C, Z), F32))
    arrive(ends)
    plane_1, plane_2 = outer_planes(zr.at[2])
    p_1 = dot(w_cf[...], halo_columns(outer, plane_1))
    p_2 = dot(w_cf[...], halo_columns(outer, plane_2))
    columns_c = halo_columns(outer, roll(plane_1, -14))
    fix = jnp.where(odd, p_1[:C], p_1[2 * C :])
    beyond = beyond + p_1[C : 2 * C] + jnp.where(odd, p_2[:C], p_2[2 * C :])
    arrive(up_sides)
    face = jnp.zeros((C, Z), F32)
    for y in range(6):
        for x in range(4):
            h, s = act_slope(fixed(outer, fix, z_e, y, x))
            own = 1 <= y < 5 and 1 <= x < 3
            up = up_grad[y - 1, x - 1] if own else up_ext[y, x].astype(F32)
            g = jnp.where(even, up * s, 0.0).astype(BF16).astype(F32)
            for a in range(3):
                if 0 <= x - a < 2:
                    g_c[y, x - a, a * C : (a + 1) * C, :] = g.astype(BF16)
            if own:
                h = jnp.where(even, h, 0.0)
                h_two[y - 1, x - 1] = jnp.concatenate([h, roll(h, 1)], axis=0).astype(BF16)
                shifted_c[y - 1, x - 1] = taps_along_z(coarse, g)
                face = add_face(coarse, face, y - 1, x - 1, jnp.where(even, g, roll(g, 1)))
    arrive(forwards)
    g_plane = planes(coarse, zr.at[1]) * act_slope(beyond)[1]
    g_plane = g_plane.astype(BF16).astype(F32)

    def long(ref):
        return jnp.concatenate([ref[y, x] for y in range(4) for x in range(2)], axis=1)

    def place(ref, row):
        chunk = ref.shape[1]
        return row // chunk, pl.ds(row % chunk, 16), slice(None)

    def store(ref, block, value):
        for at in range(0, C, 16):
            ref[place(ref, block * C + at)] = value[at : at + 16].astype(BF16)

    def pack_sums(sums, ref):
        parts = [sums[b][c * C : (c + 1) * C] for c in range(3) for b in range(3)]
        tails = [part[:, Z:] for part in parts] + [jnp.zeros((C, C), F32)]
        for j, part in enumerate(parts):
            store(ref, j, part[:, :Z])
        for q in range(5):
            store(ref, 9 + q, jnp.concatenate(tails[2 * q : 2 * q + 2], axis=1))
        for block in (18, 19):
            store(ref, block, jnp.zeros((C, Z), F32))

    in_plane = [(0, j, k) for j in range(cy) for k in range(cz) if (j, k) != (0, 0)]
    in_plane.sort(key=lambda d: -min(d[1], cy - d[1]) - min(d[2], cz - d[2]))
    in_line = sorted([(i, 0, 0) for i in range(1, cx)], key=lambda d: -min(d[0], cx - d[0]))
    plane_at = me[1] * cz + me[2]
    voxels = 4 * 8 * Z * cx * cy * cz
    scale = 1.0 / (voxels**0.5)

    def send_sum(src, dst, stage, which, n, d):
        return send(src, dst, sum_send.at[stage, which, n], sum_recv.at[stage, which, n], d)

    def scatter(which, s, ra):
        out = []
        for n, d in enumerate(in_plane):
            there = device(d)
            out.append(send_sum(s.at[there[1] * cz + there[2]], ra.at[n], 0, which, n, d))
        return out

    def along(which, s, ra, rb, waits):
        arrive(waits)
        total = s[plane_at].astype(F32)
        for n in range(len(in_plane)):
            total = total + ra[n].astype(F32)
        rb[me[0]] = total.astype(BF16)
        return [
            send_sum(rb.at[me[0]], rb.at[me[0]], 1, which, n, d) for n, d in enumerate(in_line)
        ]

    def gather(which, rb, rc, waits):
        arrive(waits)
        total = rb[0].astype(F32)
        for n in range(1, cx):
            total = total + rb[n].astype(F32)
        rc[plane_at] = (total * scale).astype(BF16)
        return [
            send_sum(rc.at[plane_at], rc.at[plane_at], 2, which, n, d)
            for n, d in enumerate(in_plane)
        ]

    inner = v_e.at[pl.ds(1, 6), pl.ds(1, 2)]
    pack_sums(filter_sum(coarse, shifted_c, face, inner, columns_c), s_a)
    p = dot_nt(long(cot), long(h_two))
    for m in range(4):
        store(s_a, 14 + m, p[m * C : (m + 1) * C])
    waits_a = scatter(0, s_a, ra_a)

    conv_rows(coarse, w_cb[...], g_c, z_c)
    fix = correction(w_cb[...], halo_columns(coarse, g_plane))
    for y in range(4):
        for x in range(2):
            g = jnp.where(even, fixed(coarse, fix, z_c, y, x) * slope_d[y, x], 0.0)
            g_two[y, x] = jnp.concatenate([g, roll(g, 1)], axis=0).astype(BF16)

    face = jnp.zeros((C, Z), F32)
    for half in range(4):
        p = dot(w_dt[...], pair(g_two, half))
        for b in range(2):
            y = half * 2 + b
            for x in range(4):
                m = b * 2 + x % 2
                wide = p[m * C : (m + 1) * C, (x // 2) * Z : (x // 2 + 1) * Z]
                c = cot[half, x // 2, m * C : (m + 1) * C, :].astype(F32)
                g = ((c + wide) * slope_f[y, x]).astype(BF16).astype(F32)
                put_own(fine, g_f, y, x, g.astype(BF16))
                shifted_f[y, x] = taps_along_z(fine, g)
                face = add_face(fine, face, y, x, g)
    pack_face(face, zs.at[3])

    pack_sums(filter_sum(fine, shifted_f, face, v_f, columns_f), s_b)
    p = dot_nt(long(g_two), long(hid))
    for c in range(2):
        for b in range(2):
            store(s_b, 14 + c * 2 + b, p[c * C : (c + 1) * C, b * Z : (b + 1) * Z])
    ends = send_ends(3, ENDS[-2:])
    waits_b = scatter(1, s_b, ra_b)
    sides = send_sides(3, fine_views(g_f))

    waits_a = along(0, s_a, ra_a, rb_a, waits_a)
    arrive(ends)
    forwards = forward_ends(3)
    waits_b = along(1, s_b, ra_b, rb_b, waits_b)
    waits_a = gather(0, rb_a, rc_a, waits_a)
    arrive(sides)
    spread_y_halo(fine, g_f)
    conv_rows(fine, w_fb[...], g_f, z_f)
    waits_b = gather(1, rb_b, rc_b, waits_b)
    arrive(forwards)
    fix = correction(w_fb[...], halo_columns(fine, planes(fine, zr.at[3])))
    for x in range(4):
        for y in range(8):
            turn[x, pl.ds(y, C, stride=8), :] = fixed(fine, fix, z_f, y, x)
        out_ref[:, x] = turn[x].reshape(C, 8, Z).astype(BF16)
    arrive(waits_a)
    a_ref[...] = rc_a[...]
    arrive(waits_b)
    b_ref[...] = rc_b[...]
    for copy in started:
        copy.wait_send()


def finish(
    field_ref, a_ref, b_ref,
    out_hbm, of_hbm, od_hbm, oc_hbm, ou_hbm,
    of_ref, od_ref, oc_ref, ou_ref,
    sems,
):
    copies = []

    def write(src, dst):
        copy = pltpu.make_async_copy(src, dst, sems.at[len(copies)])
        copy.start()
        copies.append(copy)

    write(field_ref, out_hbm)

    def load(ref, block):
        rows = []
        for at in range(block * C, (block + 1) * C, 16):
            rows.append(ref[at // ref.shape[1], pl.ds(at % ref.shape[1], 16), :])
        return jnp.concatenate(rows, axis=0).astype(F32)

    def unpack_sums(ref, o_ref):
        for block in range(14):
            value = load(ref, block)
            for half in range(2):
                j, a = (block, half) if block < 9 else (2 * (block - 9) + half, 2)
                if j < 9:
                    o_ref[a, j % 3, j // 3] = value[:, half * C : (half + 1) * C]

    unpack_sums(a_ref, oc_ref)
    write(oc_ref, oc_hbm)
    unpack_sums(b_ref, of_ref)
    write(of_ref, of_hbm)
    for m in range(4):
        value = load(a_ref, 14 + m)
        for c in range(2):
            ou_ref[m % 2, m // 2, c] = value[:, c * C : (c + 1) * C]
    write(ou_ref, ou_hbm)
    for c in range(2):
        for b in range(2):
            value = load(b_ref, 14 + c * 2 + b)
            for a in range(2):
                od_ref[a, b, c] = value[:, a * C : (a + 1) * C]
    write(od_ref, od_hbm)
    for copy in copies:
        copy.wait()


def solution(mesh):
    sizes = (mesh.shape["gx"], mesh.shape["gy"], mesh.shape["gz"])
    cx, cy, cz = sizes
    plane = cy * cz
    rows_a, rows_b = 20 * C // plane, 20 * C // plane

    def step(field, cotangent, w_fine, w_down, w_coarse, w_up):
        vmem = pl.BlockSpec(memory_space=pltpu.VMEM)
        hbm = pl.BlockSpec(memory_space=pltpu.HBM)
        three, two = (3, 3, 3, C, C), (2, 2, 2, C, C)
        packed = [jax.ShapeDtypeStruct((plane, rows, Z), BF16) for rows in (rows_a, rows_b)]
        whole = jax.ShapeDtypeStruct((C, 4, 8, Z), BF16)
        inputs = [
            pltpu.with_memory_space_constraint(v, pltpu.HBM)
            for v in (field, cotangent, w_fine, w_down, w_coarse, w_up)
        ]
        grad, sums_a, sums_b = pl.pallas_call(
            functools.partial(kernel, sizes),
            out_shape=[whole, *packed],
            in_specs=[hbm] * 6,
            out_specs=[vmem] * 3,
            scratch_shapes=[
                pltpu.VMEM((C, 4, 8, Z), BF16),
                pltpu.VMEM((C, 4, 8, Z), BF16),
                pltpu.VMEM(three, BF16),
                pltpu.VMEM(two, BF16),
                pltpu.VMEM(three, BF16),
                pltpu.VMEM(two, BF16),
                pltpu.VMEM((3 * C, 9 * C), BF16),
                pltpu.VMEM((3 * C, 9 * C), BF16),
                pltpu.VMEM((3 * C, 9 * C), BF16),
                pltpu.VMEM((3 * C, 9 * C), BF16),
                pltpu.VMEM((2 * C, 4 * C), BF16),
                pltpu.VMEM((4 * C, 2 * C), BF16),
                pltpu.VMEM((2 * C, 4 * C), BF16),
                pltpu.VMEM((10, 4, 3 * C, Z), BF16),
                pltpu.VMEM((8, 4, 3 * C, Z), BF16),
                pltpu.VMEM((6, 2, 3 * C, Z), BF16),
                pltpu.VMEM((10, 4, 3 * C, Z), BF16),
                pltpu.VMEM((8, 3, C, Z), BF16),
                pltpu.VMEM((6, 4, C, Z), BF16),
                pltpu.VMEM((4, 2, C // 2, Z), BF16),
                pltpu.VMEM((4, 9, 2, C // 2, Z), BF16),
                pltpu.VMEM((4, 8 * C, Z), F32),
                pltpu.VMEM((4, 2, 4 * C, Z), BF16),
                pltpu.VMEM((4, 2, 4 * C, Z), BF16),
                pltpu.VMEM((4, 2, C, Z), F32),
                pltpu.VMEM((8, 4, C, Z), F32),
                pltpu.VMEM((4, 2, C, Z), F32),
                pltpu.VMEM((8, 4, 3 * C, Z), BF16),
                pltpu.VMEM((4, 2, 3 * C, Z), BF16),
                pltpu.VMEM((4, 2, 2 * C, Z), BF16),
                pltpu.VMEM((4, 2, 2 * C, Z), BF16),
                pltpu.VMEM((8, 4, C, Z), F32),
                pltpu.VMEM((4, 2, C, Z), F32),
                pltpu.VMEM((6, 4, C, Z), F32),
                pltpu.VMEM((plane, rows_a, Z), BF16),
                pltpu.VMEM((plane, rows_b, Z), BF16),
                pltpu.VMEM((plane - 1, rows_a, Z), BF16),
                pltpu.VMEM((plane - 1, rows_b, Z), BF16),
                pltpu.VMEM((cx, rows_a, Z), BF16),
                pltpu.VMEM((cx, rows_b, Z), BF16),
                pltpu.VMEM((plane, rows_a, Z), BF16),
                pltpu.VMEM((plane, rows_b, Z), BF16),
                pltpu.SemaphoreType.DMA((9,)),
                pltpu.SemaphoreType.DMA((4, 8)),
                pltpu.SemaphoreType.DMA((4, 8)),
                pltpu.SemaphoreType.DMA((4, 18)),
                pltpu.SemaphoreType.DMA((4, 18)),
                pltpu.SemaphoreType.DMA((3, 2, 15)),
                pltpu.SemaphoreType.DMA((3, 2, 15)),
            ],
            compiler_params=pltpu.CompilerParams(
                collective_id=0, has_side_effects=True, vmem_limit_bytes=48 * 1024 * 1024
            ),
        )(*inputs)
        return pl.pallas_call(
            finish,
            out_shape=[whole]
            + [jax.ShapeDtypeStruct(s, F32) for s in (three, two, three, two)],
            in_specs=[vmem] * 3,
            out_specs=[hbm] * 5,
            scratch_shapes=[pltpu.VMEM(s, F32) for s in (three, two, three, two)]
            + [pltpu.SemaphoreType.DMA((5,))],
            compiler_params=pltpu.CompilerParams(vmem_limit_bytes=32 * 1024 * 1024),
        )(grad, sums_a, sums_b)

    return jax.shard_map(
        step,
        mesh=mesh,
        in_specs=(P(None, "gx", "gy", "gz"), P(None, "gx", "gy", "gz"), P(), P(), P(), P()),
        out_specs=(P(None, "gx", "gy", "gz"), P(), P(), P(), P()),
        check_vma=False,
    )
```
